128 devices in a mesh: row: 8 (over x, z_lo), col: 16 (over z_hi, y, core).
Axes of the slice: x: 4, y: 4, z: 4 (z_hi: 2, z_lo: 2; z = z_hi * 2 + z_lo), core: 2. Of those that a mesh axis runs over, the one named last changes fastest.
Arguments:
- student: bfloat16 [12288, 4096], P('col', 'row'), may hold values from -25 to 25
- teacher: bfloat16 [12288, 4096], P('col', 'row'), may hold values from -6 to 6
Outputs:
- gradient: float32 [12288, 4096], P('col', 'row')
- total_loss: float32 [], replicated
The draws below stay inside these ranges and needn't reach their ends.
All inputs are finite; a program needn't handle non-finite values.
Results may differ from the reference program's by a relative error of at most 0.0025.
Values may be sent and summed in bfloat16 or wider, within the bound.
No kernel may reach another device: no remote copies, remote signals or barrier semaphores. Data moves between devices by JAX's collectives and lax.ppermute only.
A program may use at most 128 MiB of HBM per device.

```python
import jax
import jax.numpy as jnp
from jax import lax

F = 4096
B = 12288


def draw_student(key, part):
    key = jax.random.fold_in(key, 1)
    key_scale, key_value, key_shift = jax.random.split(key, 3)
    pick = jax.random.uniform(key_scale, (F,), jnp.float32)
    scales = jnp.where(pick < 0.5, 0.3 + pick, 1.25 + 3.5 * (pick - 0.5))
    shifts = jax.random.uniform(key_shift, (F,), jnp.float32, -1.0, 1.0)
    values = jnp.clip(jax.random.normal(key_value, (B, F), jnp.float32), -7.0, 7.0)
    return (values * scales[None, :] + shifts[None, :]).astype(jnp.bfloat16)


def block_scale(key, dims, cuts, least, high):
    loudness, own = 1.0, jax.random.fold_in(key, 6)
    for axis_at, shards_of in cuts:
        steps = jnp.exp(jax.random.uniform(jax.random.fold_in(own, axis_at), (shards_of,), jnp.float32, least / len(cuts), high / len(cuts)))
        loudness = loudness * jnp.repeat(steps, dims[axis_at] // shards_of).reshape([-1 if axis == axis_at else 1 for axis in range(len(dims))])
    return loudness


def noise(stream_key, shape, deviation, bound, pieces=(), held_as=jnp.bfloat16):
    values = jax.random.normal(stream_key, shape, jnp.float32) * deviation
    if len(pieces) > 0:
        values = block_scale(stream_key, shape, pieces, -0.22, 0.18) * values
    return jnp.clip(values, min=-bound, max=bound).astype(held_as)


def setup_inputs(seed: int = 0) -> dict:
    key_list = jax.random.split(jax.random.key(seed), 3)
    return {
        "student": draw_student(jax.random.fold_in(key_list[2], 71), 0),
        "teacher": noise(key_list[1], (B, F), 1.0, 6.0, ((0, 16), (1, 8))),
    }


def reference(student, teacher):
    floats = student.astype(jnp.float32)
    target = teacher.astype(jnp.float32)
    batch = student.shape[0]
    feats = student.shape[1]
    average = lax.optimization_barrier(jnp.mean(floats, axis=0))
    centered = floats - average
    spread = jnp.sqrt(lax.optimization_barrier(jnp.sum(centered * centered, axis=0)) / (batch - 1) + 0.0001)
    centered_b = centered.astype(jnp.bfloat16)
    width = feats // 16
    row_ids = jnp.arange(feats, dtype=jnp.int32)[:, None]

    def block(block_index):
        offset = (block_index * width).astype(jnp.int32)
        columns = lax.dynamic_slice_in_dim(centered_b, offset, width, 1)
        covar = jnp.dot(centered_b.T, columns, preferred_element_type=jnp.float32) / (batch - 1)
        col_ids = offset + jnp.arange(width, dtype=jnp.int32)[None, :]
        masked = jnp.where(row_ids == col_ids, jnp.float32(0.0), covar)
        partial_value = jnp.sum(masked * masked)
        grad_part = jnp.dot(centered_b, masked.astype(jnp.bfloat16), preferred_element_type=jnp.float32)
        return (partial_value, grad_part)
    parts, grads = lax.map(block, jnp.arange(16, dtype=jnp.int32))
    cov_grad = jnp.transpose(grads, (1, 0, 2)).reshape(batch, feats)
    diff = floats - target
    total_loss = 25.0 * jnp.mean(diff * diff) + 25.0 * jnp.mean(jnp.maximum(0.0, 1.0 - spread)) + jnp.sum(parts) / feats
    hinge = jnp.where(spread < 1.0, centered / (spread * (batch - 1)), jnp.float32(0.0))
    gradient = 25.0 * diff / 32.0 - 25.0 * batch / 64.0 * hinge + batch / (16.0 * (batch - 1)) * cov_grad
    return (gradient, total_loss)
```

```python
import jax
import jax.numpy as jnp
from jax import lax
from jax.sharding import PartitionSpec as P

F32 = jnp.float32
BF16 = jnp.bfloat16

CORE_GROUPS = [[2 * chip + core for chip in range(8)] for core in range(2)]


def shift_row(block, dx, dz):
    pairs = [(2 * x + z, 2 * ((x + dx) % 4) + (z + dz) % 2) for x in range(4) for z in range(2)]
    return lax.ppermute(block, "row", pairs)


def swap_cores(block):
    return lax.ppermute(block, "col", [(i, i ^ 1) for i in range(16)])


def exchange_chips(pieces):
    return lax.all_to_all(pieces, "col", 0, 0, axis_index_groups=CORE_GROUPS)


def share(block, axes, count):
    return lax.all_to_all(jnp.broadcast_to(block[None], (count,) + block.shape), axes, 0, 0)


def per_device(student, teacher):
    images, feats = student.shape
    batch = images * 16
    half = feats // 2
    slab = feats // 8
    row_index = lax.axis_index("row")
    col_index = lax.axis_index("col")
    core = col_index % 2
    chip = col_index // 2

    own = jnp.concatenate([student, swap_cores(student)], axis=0)
    mine = lax.dynamic_slice_in_dim(own, core * half, half, 1)
    x_lo = shift_row(mine, 1, 0)
    x_hi = shift_row(mine, -1, 0)
    z_own = shift_row(mine, 0, 1)

    floats = student.astype(F32)
    sums = jnp.sum(floats, axis=0)
    dev = floats - sums / images
    squares = jnp.sum(dev * dev, axis=0)
    message = jnp.concatenate([sums.reshape(4, 128), squares.reshape(4, 128)], axis=0)
    stats = share(message, ("row", "col"), 128).reshape(8, 16, 2, feats)
    means = jnp.sum(stats[:, :, 0], axis=1) / batch
    offsets = stats[:, :, 0] / images - means[:, None]
    variances = jnp.sum(stats[:, :, 1] + images * (offsets * offsets), axis=1) / (batch - 1)
    spreads = jnp.sqrt(variances + 0.0001)
    var_sum = jnp.sum(jnp.maximum(0.0, 1.0 - spreads))
    average = lax.dynamic_index_in_dim(means, row_index, 0, keepdims=False)
    spread = lax.dynamic_index_in_dim(spreads, row_index, 0, keepdims=False)
    half_means = lax.dynamic_slice_in_dim(means, core * half, half, 1)

    def centered(block, mean):
        return (block.astype(F32) - mean).astype(BF16)

    def centered_from(block, dx, dz):
        source = (row_index // 2 + dx) % 4 * 2 + (row_index + dz) % 2
        return centered(block, lax.dynamic_index_in_dim(half_means, source, 0))

    rows = centered(own, average)

    x_far = jnp.concatenate(
        [shift_row(x_lo[:images], 1, 0), shift_row(x_hi[images:], -1, 0)], axis=0
    )
    z_lo = shift_row(z_own, 1, 0)
    z_hi = shift_row(z_own, -1, 0)
    z_far = shift_row(x_far, 0, 1)

    def covariance(columns, diagonal):
        part = lax.dot_general(
            rows, columns, (((0,), (0,)), ((), ())), preferred_element_type=F32
        ).astype(BF16)
        pieces = exchange_chips(part.reshape(8, slab, columns.shape[1]))
        covar = jnp.sum(pieces.astype(F32), axis=0) / (batch - 1)
        if diagonal:
            row_ids = chip * slab + jnp.arange(slab, dtype=jnp.int32)[:, None]
            col_ids = jnp.arange(columns.shape[1], dtype=jnp.int32)[None, :]
            on_diagonal = (col_ids < half) & (row_ids == col_ids + core * half)
            covar = jnp.where(on_diagonal, F32(0.0), covar)
        cov_part = jnp.sum(covar * covar)
        masked_b = covar.astype(BF16)
        full = exchange_chips(jnp.broadcast_to(masked_b[None], (8,) + masked_b.shape))
        return full.reshape(feats, columns.shape[1]), cov_part

    def grad_part(columns, masked_b):
        return lax.dot_general(
            columns, masked_b, (((1,), (1,)), ((), ())), preferred_element_type=F32
        )

    near = jnp.concatenate(
        [
            lax.dynamic_slice_in_dim(rows, core * half, half, 1),
            centered_from(x_lo, -1, 0),
            centered_from(x_hi, 1, 0),
            centered_from(z_own, 0, 1),
            centered_from(x_far, 2, 0),
        ],
        axis=1,
    )
    near_masked, near_part = covariance(near, True)
    far = jnp.concatenate(
        [centered_from(z_lo, -1, 1), centered_from(z_hi, 1, 1), centered_from(z_far, 2, 1)], axis=1
    )
    far_masked, far_part = covariance(far, False)
    grads = grad_part(near, near_masked) + grad_part(far, far_masked)
    cov_grad = grads[:images] + swap_cores(grads[images:].astype(BF16)).astype(F32)

    diff = floats - teacher.astype(F32)
    inv_part = jnp.sum(diff * diff)
    lanes = jnp.arange(128, dtype=jnp.int32)[None, :]
    parts = jnp.where(lanes == 0, near_part + far_part, jnp.where(lanes == 1, inv_part, F32(0.0)))
    totals = jnp.sum(share(parts, ("row", "col"), 128), axis=(0, 1))
    cov_sum, inv_sum = totals[0], totals[1]
    total_feats = 8 * feats
    total_loss = (
        25.0 * inv_sum / (batch * total_feats)
        + 25.0 * var_sum / total_feats
        + cov_sum / total_feats
    )
    hinge = jnp.where(spread < 1.0, (floats - average) / (spread * (batch - 1)), F32(0.0))
    gradient = (
        25.0 * diff / 32.0 - 25.0 * batch / 64.0 * hinge + batch / (16.0 * (batch - 1)) * cov_grad
    )
    return (gradient, total_loss)


def solution(mesh):
    in_specs = (P("col", "row"), P("col", "row"))
    out_specs = (P("col", "row"), P())
    return jax.shard_map(
        per_device, mesh=mesh, in_specs=in_specs, out_specs=out_specs, check_vma=False
    )
```

```python
import functools

import jax
import jax.numpy as jnp
from jax import lax
from jax.experimental import pallas as pl
from jax.experimental.pallas import tpu as pltpu
from jax.sharding import PartitionSpec as P

F32 = jnp.float32
BF16 = jnp.bfloat16
IMAGES, FEATS, CHIPS = 768, 512, 8
BATCH = IMAGES * 16
CHIP_IMAGES = 2 * IMAGES
HALF = FEATS // 2
SLAB = FEATS // CHIPS
STAT_ROWS = 16

CORE_GROUPS = [[2 * chip + core for chip in range(CHIPS)] for core in range(2)]
VMEM = pl.BlockSpec(memory_space=pltpu.VMEM)
SMEM = pl.BlockSpec(memory_space=pltpu.SMEM)


def shift_row(block, dx, dz):
    pairs = [(2 * x + z, 2 * ((x + dx) % 4) + (z + dz) % 2) for x in range(4) for z in range(2)]
    return lax.ppermute(block, "row", pairs)


def swap_cores(block):
    return lax.ppermute(block, "col", [(i, i ^ 1) for i in range(16)])


def exchange_chips(pieces):
    return lax.all_to_all(pieces, "col", 0, 0, axis_index_groups=CORE_GROUPS)


def share(block, axes, count):
    return lax.all_to_all(jnp.broadcast_to(block[None], (count,) + block.shape), axes, 0, 0)


def call(body, outs, ins, scratch, flops, name):
    specs = [SMEM if a.dtype == jnp.int32 else VMEM for a in ins]
    moved = sum(a.size * a.dtype.itemsize for a in list(ins) + list(outs))
    return pl.pallas_call(
        body,
        out_shape=tuple(jax.ShapeDtypeStruct(a.shape, a.dtype) for a in outs),
        in_specs=specs,
        out_specs=tuple(VMEM for _ in outs),
        scratch_shapes=scratch,
        compiler_params=pltpu.CompilerParams(vmem_limit_bytes=48 * 2**20),
        cost_estimate=pl.CostEstimate(flops=flops, bytes_accessed=moved, transcendentals=0),
        name=name,
    )(*ins)


def shape(dims, dtype):
    return jax.ShapeDtypeStruct(dims, dtype)


def layout(chunks):
    places, column, at = [], 0, 0
    while at < len(chunks):
        rows, width = chunks[at].shape
        count = CHIP_IMAGES // rows
        for part in range(count):
            places.append((at + part, part * rows, column))
        column += width
        at += count
    return places, column


def split3(value):
    high = value.astype(BF16).astype(F32)
    middle = (value - high).astype(BF16).astype(F32)
    return [high, middle, value - high - middle]


def column_sum(ref):
    ones = jnp.ones((8, ref.shape[0]), BF16)
    return jnp.dot(ones, ref[...], preferred_element_type=F32)[0:1]


def center_into(target, first, column, ref, mean):
    width = ref.shape[1]
    step = 128

    def body(i, carry):
        at = pl.multiple_of(i * step, step)
        block = ref[pl.ds(at, step), :].astype(F32) - mean
        target[pl.ds(first + at, step), column:column + width] = block.astype(BF16)
        return carry

    lax.fori_loop(0, ref.shape[0] // step, body, 0)


def fill_columns(places, refs, columns, stats):
    means = {}
    for at, _, column in places:
        means[column] = means.get(column, 0.0) + column_sum(refs[at])
    for column, total in means.items():
        mean = total / CHIP_IMAGES
        stats[0:1, column:column + mean.shape[1]] = mean
        means[column] = mean
    for at, first, column in places:
        center_into(columns, first, column, refs[at], means[column])


def write_message(message, rows_t, columns, stats, row_mean, width):
    for piece in range(CHIPS):
        part = jnp.dot(
            rows_t[piece * SLAB:(piece + 1) * SLAB, :], columns[...], preferred_element_type=F32
        )
        message[piece, 0:SLAB, :] = part.astype(BF16)
    lines = split3(stats[0:1, :])
    if row_mean is not None:
        pad = jnp.zeros((1, width - FEATS), F32)
        lines += [jnp.concatenate([line, pad], axis=1) for line in split3(row_mean)]
    lines.append(jnp.zeros((STAT_ROWS - len(lines), width), F32))
    block = jnp.concatenate(lines, axis=0).astype(BF16)
    for piece in range(CHIPS):
        message[piece, SLAB:SLAB + STAT_ROWS, :] = block


def near_kernel(places, width, count, *refs):
    own, sibling = refs[0], refs[1]
    chunks = refs[2:2 + count]
    message, rows_t, rows, columns, stats = refs[2 + count:]
    row_mean = (column_sum(own) + column_sum(sibling)) / CHIP_IMAGES
    center_into(rows, 0, 0, own, row_mean)
    center_into(rows, IMAGES, 0, sibling, row_mean)
    for at in range(0, FEATS, 128):
        rows_t[at:at + 128, :] = rows[:, at:at + 128].T
    fill_columns(places, chunks, columns, stats)
    write_message(message, rows_t, columns, stats, row_mean, width)


def later_kernel(places, width, count, *refs):
    rows_t = refs[0]
    chunks = refs[1:1 + count]
    message, columns, stats = refs[1 + count:]
    fill_columns(places, chunks, columns, stats)
    write_message(message, rows_t, columns, stats, None, width)


def partial_near(own, sibling, chunks):
    places, width = layout(chunks)
    return call(
        functools.partial(near_kernel, places, width, len(chunks)),
        [shape((CHIPS, SLAB + STAT_ROWS, width), BF16), shape((FEATS, CHIP_IMAGES), BF16)],
        [own, sibling] + chunks,
        [
            pltpu.VMEM((CHIP_IMAGES, FEATS), BF16),
            pltpu.VMEM((CHIP_IMAGES, width), BF16),
            pltpu.VMEM((8, width), F32),
        ],
        2 * CHIP_IMAGES * FEATS * width,
        "partial_near",
    )


def partial_later(rows_t, chunks, name):
    places, width = layout(chunks)
    return call(
        functools.partial(later_kernel, places, width, len(chunks)),
        [shape((CHIPS, SLAB + STAT_ROWS, width), BF16)],
        [rows_t] + chunks,
        [pltpu.VMEM((CHIP_IMAGES, width), BF16), pltpu.VMEM((8, width), F32)],
        2 * CHIP_IMAGES * FEATS * width,
        name,
    )[0]


def combine(place, received, masked, part, means, offsets, row_offsets):
    total = jnp.zeros((SLAB, received.shape[2]), F32)
    lines = []
    for chip in range(CHIPS):
        total = total + received[chip, 0:SLAB, :].astype(F32)
        stats = received[chip, SLAB:SLAB + STAT_ROWS, :].astype(F32)
        lines.append(stats[0:1] + stats[1:2] + stats[2:3])
    local = jnp.concatenate(lines, axis=0)
    mean = jnp.sum(local, axis=0, keepdims=True) / CHIPS
    means[...] = jnp.broadcast_to(mean, means.shape)
    offsets[...] = lax.dot_general(
        row_offsets[...],
        local - mean,
        (((0,), (0,)), ((), ())),
        precision=lax.Precision.HIGHEST,
        preferred_element_type=F32,
    )
    first = pl.multiple_of(place[0] % 2 * SLAB, SLAB)
    covar = (total + CHIP_IMAGES * offsets[pl.ds(first, SLAB), :]) / (BATCH - 1)
    return covar


def finish(covar, masked, part):
    part[...] = jnp.broadcast_to(jnp.sum(covar * covar, keepdims=True), part.shape)
    masked_b = covar.astype(BF16)
    for piece in range(CHIPS):
        masked[piece] = masked_b


def combine_near_kernel(place, received, masked, part, means, row_offsets, offsets, all_rows):
    lines = []
    for chip in range(CHIPS):
        stats = received[chip, SLAB:SLAB + STAT_ROWS, 0:FEATS].astype(F32)
        lines.append(stats[3:4] + stats[4:5] + stats[5:6])
    local = jnp.concatenate(lines, axis=0)
    all_rows[...] = local - jnp.sum(local, axis=0, keepdims=True) / CHIPS
    block = pl.multiple_of(place[0] // 2 * 128, 128)
    row_offsets[...] = all_rows[:, pl.ds(block, 128)]
    covar = combine(place, received, masked, part, means, offsets, row_offsets)
    row_ids = place[0] * SLAB + lax.broadcasted_iota(jnp.int32, covar.shape, 0)
    col_ids = lax.broadcasted_iota(jnp.int32, covar.shape, 1)
    on_diagonal = (col_ids < HALF) & (row_ids == col_ids + place[1] * HALF)
    finish(jnp.where(on_diagonal, F32(0.0), covar), masked, part)


def combine_later_kernel(place, received, row_offsets, masked, part, means, offsets):
    covar = combine(place, received, masked, part, means, offsets, row_offsets)
    finish(covar, masked, part)


def combined(place, received, row_offsets, name):
    width = received.shape[2]
    outs = [
        shape((CHIPS, SLAB, width), BF16),
        shape((8, 128), F32),
        shape((8, width), F32),
    ]
    scratch = [pltpu.VMEM((128, width), F32)]
    flops = 24 * SLAB * width
    if row_offsets is None:
        outs.append(shape((8, 128), F32))
        scratch.append(pltpu.VMEM((8, FEATS), F32))
        return call(combine_near_kernel, outs, [place, received], scratch, flops, name)
    return call(
        combine_later_kernel, outs, [place, received, row_offsets], scratch, flops, name
    )


def grad_kernel(places, count, first, rows, with_sum, kind, *refs):
    chunks = refs[:count]
    means, masked = refs[count], refs[count + 1]
    rest = refs[count + 2:]
    previous = rest[0] if with_sum else None
    out, columns = rest[-2], rest[-1]
    width = masked.shape[1]
    step = 256
    for at in range(first, first + rows, step):
        for index, start, column in places:
            chunk = chunks[index]
            if start <= at < start + chunk.shape[0]:
                span = chunk.shape[1]
                block = chunk[at - start:at - start + step, :].astype(F32)
                block = block - means[0:1, column:column + span]
                columns[:, column:column + span] = block.astype(BF16)
        product = lax.dot_general(
            columns[...], masked[...], (((1,), (1,)), ((), ())), preferred_element_type=F32
        )
        if with_sum:
            product = product + previous[at:at + step, :]
        out[at - first:at - first + step, :] = product.astype(out.dtype)


def grad_part(chunks, means, masked, previous, first, rows, dtype, name):
    places, width = layout(chunks)
    ins = list(chunks) + [means, masked] + ([previous] if previous is not None else [])
    return call(
        functools.partial(
            grad_kernel, places, len(chunks), first, rows, previous is not None, None
        ),
        [shape((rows, FEATS), dtype)],
        ins,
        [pltpu.VMEM((256, width), BF16)],
        2 * rows * FEATS * width,
        name,
    )[0]


def per_device(student, teacher):
    row_index = lax.axis_index("row")
    col_index = lax.axis_index("col")
    core = col_index % 2
    place = jnp.stack([col_index // 2, core]).astype(jnp.int32)

    sibling = swap_cores(student)
    own_a = lax.dynamic_slice_in_dim(student, core * HALF, HALF, 1)
    x_lo_a = shift_row(own_a, 1, 0)
    x_hi_a = shift_row(own_a, -1, 0)
    z_own_a = shift_row(own_a, 0, 1)
    own_b = lax.dynamic_slice_in_dim(sibling, core * HALF, HALF, 1)
    x_lo_b = shift_row(own_b, 1, 0)
    x_hi_b = shift_row(own_b, -1, 0)
    z_own_b = shift_row(own_b, 0, 1)
    x_far_a = shift_row(x_lo_a, 1, 0)
    x_far_b = shift_row(x_hi_b, -1, 0)
    z_own_0 = jnp.concatenate([z_own_a[:, :128], z_own_b[:, :128]], axis=0)
    z_own_1 = jnp.concatenate([z_own_a[:, 128:], z_own_b[:, 128:]], axis=0)
    z_lo_0 = shift_row(z_own_0, 1, 0)
    z_hi_0 = shift_row(z_own_0, -1, 0)
    z_lo_1 = shift_row(z_own_1, 1, 0)
    z_hi_1 = shift_row(z_own_1, -1, 0)
    x_far_0 = jnp.concatenate([x_far_a[:, :128], x_far_b[:, :128]], axis=0)
    x_far_1 = jnp.concatenate([x_far_a[:, 128:], x_far_b[:, 128:]], axis=0)
    z_far_0 = shift_row(x_far_0, 0, 1)
    z_far_1 = shift_row(x_far_1, 0, 1)

    near = [own_a, own_b, x_lo_a, x_lo_b, x_hi_a, x_hi_b, z_own_a, z_own_b]
    middle = [x_far_a, x_far_b, z_lo_0, z_hi_0, z_far_0]
    far = [z_lo_1, z_hi_1, z_far_1]

    near_sums, rows_t = partial_near(student, sibling, near)
    near_received = exchange_chips(near_sums)
    middle_received = exchange_chips(partial_later(rows_t, middle, "partial_middle"))
    far_received = exchange_chips(partial_later(rows_t, far, "partial_far"))

    near_masked, near_part, near_means, row_offsets = combined(
        place, near_received, None, "combine_near"
    )
    middle_masked, middle_part, middle_means = combined(
        place, middle_received, row_offsets, "combine_middle"
    )
    far_masked, far_part, far_means = combined(place, far_received, row_offsets, "combine_far")
    near_all = exchange_chips(near_masked).reshape(FEATS, -1)
    middle_all = exchange_chips(middle_masked).reshape(FEATS, -1)
    far_all = exchange_chips(far_masked).reshape(FEATS, -1)

    floats = student.astype(F32)
    sums = jnp.sum(floats, axis=0)
    dev = floats - sums / IMAGES
    squares = jnp.sum(dev * dev, axis=0)
    message = jnp.concatenate([sums.reshape(4, 128), squares.reshape(4, 128)], axis=0)
    stats = lax.all_gather(message, "col").reshape(16, 2, FEATS)
    average = jnp.sum(stats[:, 0], axis=0) / BATCH
    shift = stats[:, 0] / IMAGES - average
    variance = jnp.sum(stats[:, 1] + IMAGES * (shift * shift), axis=0) / (BATCH - 1)
    spread = jnp.sqrt(variance + 0.0001)
    var_part = jnp.sum(jnp.maximum(0.0, 1.0 - spread)) / 16
    diff = floats - teacher.astype(F32)
    inv_part = jnp.sum(diff * diff)
    hinge = jnp.where(spread < 1.0, (floats - average) / (spread * (BATCH - 1)), F32(0.0))
    base = lax.optimization_barrier(25.0 * diff / 32.0 - 25.0 * BATCH / 64.0 * hinge)

    cov_part = near_part[0, 0] + middle_part[0, 0] + far_part[0, 0]
    lanes = jnp.arange(128, dtype=jnp.int32)[None, :]
    parts = jnp.where(
        lanes == 0, cov_part, jnp.where(lanes == 1, inv_part, jnp.where(lanes == 2, var_part, 0.0))
    )
    totals = jnp.sum(share(parts, ("row", "col"), 128), axis=(0, 1))

    grads = grad_part(near, near_means, near_all, None, 0, CHIP_IMAGES, F32, "grad_near")
    grads = grad_part(middle, middle_means, middle_all, grads, 0, CHIP_IMAGES, F32, "grad_middle")
    outgoing = grad_part(far, far_means, far_all, grads, IMAGES, IMAGES, BF16, "grad_far_sent")
    outgoing, totals = lax.optimization_barrier((outgoing, totals))
    incoming = swap_cores(outgoing)
    kept = grad_part(far, far_means, far_all, grads, 0, IMAGES, F32, "grad_far_kept")

    cov_sum, inv_sum, var_sum = totals[0], totals[1], totals[2]
    total_feats = 8 * FEATS
    total_loss = (
        25.0 * inv_sum / (BATCH * total_feats)
        + 25.0 * var_sum / total_feats
        + cov_sum / total_feats
    )
    gradient = base + BATCH / (16.0 * (BATCH - 1)) * (kept + incoming.astype(F32))
    return (gradient, total_loss)


def solution(mesh):
    in_specs = (P("col", "row"), P("col", "row"))
    out_specs = (P("col", "row"), P())
    return jax.shard_map(
        per_device, mesh=mesh, in_specs=in_specs, out_specs=out_specs, check_vma=False
    )
```

```python
import functools

import jax
import jax.numpy as jnp
from jax import lax
from jax.experimental import pallas as pl
from jax.experimental.pallas import tpu as pltpu
from jax.sharding import PartitionSpec as P

F32 = jnp.float32
BF16 = jnp.bfloat16
IMAGES, FEATS, CHIPS = 768, 512, 8
BATCH = IMAGES * 16
CHIP_IMAGES = 2 * IMAGES
HALF = FEATS // 2
STAT_ROWS = 16

QUARTER = FEATS // 4
VMEM = pl.BlockSpec(memory_space=pltpu.VMEM)
SMEM = pl.BlockSpec(memory_space=pltpu.SMEM)
ANY = pl.BlockSpec(memory_space=pl.ANY)


def shift_row(block, dx, dz):
    pairs = [(2 * x + z, 2 * ((x + dx) % 4) + (z + dz) % 2) for x in range(4) for z in range(2)]
    return lax.ppermute(block, "row", pairs)


def swap_cores(block):
    return lax.ppermute(block, "col", [(i, i ^ 1) for i in range(16)])


def shift_y(block, dy):
    pairs = [
        (8 * z + 2 * y + core, 8 * z + 2 * ((y + dy) % 4) + core)
        for z in range(2) for y in range(4) for core in range(2)
    ]
    return lax.ppermute(block, "col", pairs)


def swap_z_hi(block):
    return lax.ppermute(block, "col", [(i, i ^ 8) for i in range(16)])


def call(body, outs, ins, scratch, name, after=(), flops=0):
    count, waits = len(ins), len(after)

    def kernel(*refs):
        body(*refs[:count], *refs[count + waits:])

    return pl.pallas_call(
        kernel,
        out_shape=tuple(outs),
        in_specs=[SMEM if a.dtype == jnp.int32 else VMEM for a in ins] + [ANY] * waits,
        out_specs=tuple(VMEM for _ in outs),
        scratch_shapes=scratch,
        compiler_params=pltpu.CompilerParams(vmem_limit_bytes=26 * 2**20),
        cost_estimate=pl.CostEstimate(flops=flops, bytes_accessed=0, transcendentals=0),
        name=name,
    )(*ins, *after)


def shape(dims, dtype):
    return jax.ShapeDtypeStruct(dims, dtype)


def layout(chunks):
    places, column, at = [], 0, 0
    while at < len(chunks):
        rows, width = chunks[at].shape
        count = CHIP_IMAGES // rows
        for part in range(count):
            places.append((at + part, part * rows, column))
        column += width
        at += count
    return places, column


def split3(value):
    high = value.astype(BF16).astype(F32)
    middle = (value - high).astype(BF16).astype(F32)
    return [high, middle, value - high - middle]


def column_sum(ref):
    ones = jnp.ones((8, ref.shape[0]), BF16)
    return jnp.dot(ones, ref[...], preferred_element_type=F32)[0:1]


def center_into(target, first, column, ref, mean):
    width = ref.shape[1]
    step = 128

    def body(i, carry):
        at = pl.multiple_of(i * step, step)
        block = ref[pl.ds(at, step), :].astype(F32) - mean
        target[pl.ds(first + at, step), column:column + width] = block.astype(BF16)
        return carry

    lax.fori_loop(0, ref.shape[0] // step, body, 0)


def fill_columns(places, refs, columns, stats):
    means = {}
    for at, _, column in places:
        means[column] = means.get(column, 0.0) + column_sum(refs[at])
    for column, total in means.items():
        mean = total / CHIP_IMAGES
        stats[0:1, column:column + mean.shape[1]] = mean
        means[column] = mean
    for at, first, column in places:
        center_into(columns, first, column, refs[at], means[column])


def center_rows(target, first, ref, mean):
    step = 128

    def body(i, total):
        at = pl.multiple_of(i * step, step)
        block = ref[pl.ds(at, step), :].astype(F32) - mean
        target[pl.ds(first + at, step), :] = block.astype(BF16)
        return total + jnp.sum((block * block).reshape(step // 8, 8, FEATS), axis=0)

    total = lax.fori_loop(0, ref.shape[0] // step, body, jnp.zeros((8, FEATS), F32))
    return jnp.sum(total, axis=0, keepdims=True)


def padded(lines, width):
    pad = width - lines[0].shape[1]
    return [jnp.concatenate([line, jnp.zeros((line.shape[0], pad), F32)], axis=1) for line in lines]


def filled(lines, width):
    count = sum(line.shape[0] for line in lines)
    lines = lines + [jnp.zeros((-count % STAT_ROWS, width), F32)]
    return jnp.concatenate([line for line in lines if line.shape[0]], axis=0)


def rows_kernel(own, sibling, rows_t, row_stats, rows):
    row_mean = (column_sum(own) + column_sum(sibling)) / CHIP_IMAGES
    squares = center_rows(rows, 0, own, row_mean) + center_rows(rows, IMAGES, sibling, row_mean)
    for at in range(0, FEATS, 128):
        rows_t[at:at + 128, :] = rows[:, at:at + 128].T
    row_stats[...] = jnp.concatenate([row_mean, squares, jnp.zeros((6, FEATS), F32)], axis=0)


def center_own(own, sibling):
    return call(
        rows_kernel,
        [shape((FEATS, CHIP_IMAGES), BF16), shape((8, FEATS), F32)],
        [own, sibling],
        [pltpu.VMEM((CHIP_IMAGES, FEATS), BF16)],
        "center_own",
    )


def products(rows_t, columns, at, step):
    return jnp.dot(rows_t[...], columns[:, at:at + step], preferred_element_type=F32)


def partial_kernel(places, width, count, with_rows, *refs):
    place, rows_t, row_stats = refs[:3]
    chunks = refs[3:3 + count]
    pieces = refs[3 + count:7 + count]
    columns, stats, sums = refs[7 + count:]
    fill_columns(places, chunks, columns, stats)
    for at in range(0, width, 256):
        sums[:, at:at + 256] = jnp.dot(
            rows_t[...], columns[:, at:at + 256], preferred_element_type=F32
        )
    lines = split3(stats[0:1, :])
    if with_rows:
        lines += padded(split3(row_stats[0:1, :]) + split3(row_stats[1:2, :]), width)
    block = filled(lines, width)
    for d in range(4):
        first = pl.multiple_of((place[2] + d) % 4 * QUARTER, QUARTER)
        pieces[d][0:QUARTER, :] = sums[pl.ds(first, QUARTER), :].astype(pieces[d].dtype)
        pieces[d][QUARTER:QUARTER + STAT_ROWS, :] = block.astype(pieces[d].dtype)


def partial_sums(place, rows_t, row_stats, chunks, with_rows, name, after=()):
    places, width = layout(chunks)
    rows = QUARTER + STAT_ROWS
    *pieces, columns, stats = call(
        functools.partial(partial_kernel, places, width, len(chunks), with_rows),
        [shape((rows, width), F32)]
        + [shape((rows, width), BF16)] * 3
        + [shape((CHIP_IMAGES, width), BF16), shape((8, width), F32)],
        [place, rows_t, row_stats] + chunks,
        [pltpu.VMEM((FEATS, width), F32)],
        name,
        after,
        flops=2 * CHIP_IMAGES * FEATS * width,
    )
    return pieces, columns, stats


def spread_out(local):
    mean = jnp.sum(local, axis=0, keepdims=True) / CHIPS
    return local - mean, mean


def mean_term(row_offsets, col_offsets):
    return CHIP_IMAGES * lax.dot_general(
        row_offsets,
        col_offsets,
        (((0,), (0,)), ((), ())),
        precision=lax.Precision.HIGHEST,
        preferred_element_type=F32,
    )


def three(stats, first):
    return stats[first:first + 1] + stats[first + 1:first + 2] + stats[first + 2:first + 3]


def combine_y_kernel(with_rows, place, own, one, two, three_on, plane, message, local, *row_local):
    width = own.shape[1]
    columns = jnp.zeros((4, width), F32)
    rows = jnp.zeros((4, FEATS), F32)
    squares = jnp.zeros((1, FEATS), F32)
    total = own[0:QUARTER, :]
    for d, piece in enumerate((own, one, two, three_on)):
        if d:
            total = total + piece[0:QUARTER, :].astype(F32)
        at = (place[2] + 4 - d) % 4
        stats = piece[QUARTER:QUARTER + STAT_ROWS, :].astype(F32)
        here = lax.broadcasted_iota(jnp.int32, columns.shape, 0) == at
        columns = jnp.where(here, three(stats, 0), columns)
        if with_rows:
            here = lax.broadcasted_iota(jnp.int32, rows.shape, 0) == at
            rows = jnp.where(here, three(stats[:, 0:FEATS], 3), rows)
            squares = squares + three(stats[:, 0:FEATS], 6)

    def rounded(value):
        high, middle, low = split3(value)
        low = low.astype(BF16).astype(F32)
        return [high, middle, low], high + middle + low

    plane[...] = total.astype(BF16)
    message[0:QUARTER, :] = total.astype(BF16)
    lines, local[0:4, :] = rounded(columns)
    if with_rows:
        row_lines, row_local[0][0:4, :] = rounded(rows)
        square_lines, row_local[0][4:5, :] = rounded(squares)
        lines = lines + padded(row_lines + square_lines, width)
    block = filled(lines, width)
    message[QUARTER:QUARTER + block.shape[0], :] = block.astype(BF16)


def combine_y(place, pieces, with_rows, name, after):
    width = pieces[0].shape[1]
    rows = QUARTER + (2 if with_rows else 1) * STAT_ROWS
    outs = [shape((QUARTER, width), BF16), shape((rows, width), BF16), shape((8, width), F32)]
    outs += [shape((8, FEATS), F32)] if with_rows else []
    return call(
        functools.partial(combine_y_kernel, with_rows), outs, [place] + pieces, [], name, after
    )


def all_chips(place, mine, theirs):
    low = place[3] == 0
    return jnp.concatenate([jnp.where(low, mine, theirs), jnp.where(low, theirs, mine)], axis=0)


def combine_z_kernel(
    with_rows, place, plane, local, rows, received, parts, masked, part, means, *more
):
    stats = received[QUARTER:, :].astype(F32)
    theirs = stats[0:4] + stats[4:8] + stats[8:12]
    col_off, col_mean = spread_out(all_chips(place, local[0:4, :], theirs))
    means[...] = jnp.broadcast_to(col_mean, means.shape)
    row_offsets = rows
    if with_rows:
        row_offsets, row_stats = more
        stats = stats[:, 0:FEATS]
        theirs = stats[12:16] + stats[16:20] + stats[20:24]
        row_off, row_mean = spread_out(all_chips(place, rows[0:4, :], theirs))
        squares = rows[4:5, :] + three(stats, 24)
        squares = squares + CHIP_IMAGES * jnp.sum(row_off * row_off, axis=0, keepdims=True)
        variance = squares / (BATCH - 1)
        row_offsets[...] = row_off
        row_stats[...] = jnp.concatenate([row_mean, variance, jnp.zeros((6, FEATS), F32)], axis=0)
    block = pl.multiple_of(place[2] * QUARTER, QUARTER)
    term = mean_term(row_offsets[:, pl.ds(block, QUARTER)], col_off)
    covar = plane[...].astype(F32) + received[0:QUARTER, :].astype(F32)
    covar = (covar + term) / (BATCH - 1)
    if with_rows:
        row_ids = place[2] * QUARTER + lax.broadcasted_iota(jnp.int32, covar.shape, 0)
        col_ids = lax.broadcasted_iota(jnp.int32, covar.shape, 1)
        on_diagonal = (col_ids < HALF) & (row_ids == col_ids + place[1] * HALF)
        covar = jnp.where(on_diagonal, F32(0.0), covar)
    lanes = lax.broadcasted_iota(jnp.int32, part.shape, 1)
    part[...] = parts[...] + jnp.where(lanes == 0, jnp.sum(covar * covar, keepdims=True), 0.0)
    masked[0:QUARTER, :] = covar.astype(BF16)
    if not with_rows:
        block = filled(padded(split3(part[0:1, :]), covar.shape[1]), covar.shape[1])
        masked[QUARTER:QUARTER + STAT_ROWS, :] = block.astype(BF16)


def combine_z(place, plane, local, rows, received, parts, with_rows, name, after=()):
    width = plane.shape[1]
    count = QUARTER + (0 if with_rows else STAT_ROWS)
    outs = [shape((count, width), BF16), shape((8, 128), F32), shape((8, width), F32)]
    outs += [shape((8, FEATS), F32)] * 2 if with_rows else []
    ins = [place, plane, local, rows, received, parts]
    return call(functools.partial(combine_z_kernel, with_rows), outs, ins, [], name, after)


def parts_kernel(place, own, one, two, three_on, out):
    lines = jnp.zeros((4, 128), F32)
    for d, piece in enumerate((own, one, two, three_on)):
        here = lax.broadcasted_iota(jnp.int32, lines.shape, 0) == (place[2] + 4 - d) % 4
        lines = jnp.where(here, three(piece[QUARTER:, 0:128].astype(F32), 0), lines)
    out[...] = jnp.broadcast_to(jnp.sum(lines, axis=0, keepdims=True), out.shape)


def sum_parts(place, pieces, after):
    return call(
        parts_kernel, [shape((8, 128), F32)], [place] + pieces, [], "sum_parts", after
    )[0]


def shift_term(stats, means, masked):
    lines = filled(split3(stats[0:1, :] - means[0:1, :]), stats.shape[1]).astype(BF16)
    rows = lax.dot_general(
        lines, masked[...], (((1,), (1,)), ((), ())), preferred_element_type=F32
    )
    return rows[0:1] + rows[1:2] + rows[2:3]


def times_masked(columns, at, masked):
    return lax.dot_general(
        columns[at:at + 256, :], masked[...], (((1,), (1,)), ((), ())), preferred_element_type=F32
    )


def grad_kernel(
    first, rows, add, place, columns, stats, means, own, one, two, three_on, *rest
):
    out, masked = rest[-2:]
    for d, piece in enumerate((own, one, two, three_on)):
        row = pl.multiple_of((place[2] + 4 - d) % 4 * QUARTER, QUARTER)
        masked[pl.ds(row, QUARTER), :] = piece[0:QUARTER, :]
    shift = shift_term(stats, means, masked)
    for at in range(first, first + rows, 256):
        product = times_masked(columns, at, masked) + shift
        if add:
            product = product + rest[0][at:at + 256, :]
        out[at - first:at - first + 256, :] = product.astype(out.dtype)


def grad_part(place, inputs, pieces, previous, first, rows, dtype, name, after=()):
    columns, stats, means = inputs
    ins = [place, columns, stats, means] + pieces + ([] if previous is None else [previous])
    return call(
        functools.partial(grad_kernel, first, rows, previous is not None),
        [shape((rows, FEATS), dtype)],
        ins,
        [pltpu.VMEM((FEATS, columns.shape[1]), BF16)],
        name,
        after,
    )[0]


def per_device(student, teacher):
    row_index = lax.axis_index("row")
    col_index = lax.axis_index("col")
    core = col_index % 2
    chip = col_index // 2
    place = jnp.stack([chip, core, chip % 4, chip // 4]).astype(jnp.int32)

    sibling = swap_cores(student)
    own_a = lax.dynamic_slice_in_dim(student, core * HALF, HALF, 1)
    x_lo_a = shift_row(own_a, 1, 0)
    x_hi_a = shift_row(own_a, -1, 0)
    z_own_a = shift_row(own_a, 0, 1)
    own_b = lax.dynamic_slice_in_dim(sibling, core * HALF, HALF, 1)
    x_lo_b = shift_row(own_b, 1, 0)
    x_hi_b = shift_row(own_b, -1, 0)
    z_own_b = shift_row(own_b, 0, 1)
    x_far_a = shift_row(x_lo_a, 1, 0)
    x_far_b = shift_row(x_hi_b, -1, 0)
    z_lo_a = shift_row(z_own_a, 1, 0)
    z_hi_a = shift_row(z_own_a, -1, 0)
    z_lo_b = shift_row(z_own_b, 1, 0)
    z_hi_b = shift_row(z_own_b, -1, 0)
    z_far_a = shift_row(x_far_a, 0, 1)
    z_far_b = shift_row(x_far_b, 0, 1)
    near = [own_a, own_b, x_lo_a, x_lo_b, x_hi_a, x_hi_b, z_own_a, z_own_b]

    rows_t, own_stats = center_own(student, sibling)
    near_sums, near_columns, near_stats = partial_sums(
        place, rows_t, own_stats, near, True, "partial_near", [x_far_a]
    )
    near_sums, z_lo_a, z_hi_a = lax.optimization_barrier((near_sums, z_lo_a, z_hi_a))
    far = [x_far_a, x_far_b, z_lo_a, z_lo_b, z_hi_a, z_hi_b, z_far_a, z_far_b]
    near_sums[1:] = [shift_y(near_sums[d], d) for d in (1, 2, 3)]
    far_sums, far_columns, far_stats = partial_sums(
        place, rows_t, own_stats, far, False, "partial_far"
    )
    far_sums[1:] = [shift_y(far_sums[d], d) for d in (1, 2, 3)]

    floats = student.astype(F32)
    diff = floats - teacher.astype(F32)
    lanes = lax.broadcasted_iota(jnp.int32, (8, 128), 1)
    parts = jnp.where(lanes == 1, jnp.sum(diff * diff), F32(0.0))
    parts = parts + swap_z_hi(parts)

    plane, message, local, row_local = combine_y(
        place, near_sums, True, "combine_y_near", [far_sums[0]]
    )
    near_masked, parts, near_means, row_offsets, row_stats = combine_z(
        place, plane, local, row_local, swap_z_hi(message), parts, True, "combine_z_near"
    )
    near_pieces = [near_masked] + [shift_y(near_masked, d) for d in (1, 2, 3)]
    average = row_stats[0]
    spread = jnp.sqrt(row_stats[1] + 0.0001)
    hinge = jnp.where(spread < 1.0, (floats - average) / (spread * (BATCH - 1)), F32(0.0))
    base = lax.optimization_barrier(25.0 * diff / 32.0 - 25.0 * BATCH / 64.0 * hinge)
    var_part = jnp.sum(jnp.maximum(0.0, 1.0 - spread)) / 8
    parts = jnp.where(lanes == 2, var_part, parts)

    plane, message, local = combine_y(place, far_sums, False, "combine_y_far", [near_masked])
    far_masked, _, far_means = combine_z(
        place, plane, local, row_offsets, swap_z_hi(message), parts, False, "combine_z_far"
    )
    far_pieces = [far_masked] + [shift_y(far_masked, d) for d in (1, 2, 3)]

    near_inputs = (near_columns, near_stats, near_means)
    far_inputs = (far_columns, far_stats, far_means)
    grads = grad_part(
        place, near_inputs, near_pieces, None, 0, CHIP_IMAGES, F32, "grad_near", [base]
    )
    parts = sum_parts(place, far_pieces, [grads])
    steps = [parts]
    for axis, bit in (("row", 2), ("row", 4), ("row", 1), ("col", 1)):
        size = 8 if axis == "row" else 16
        parts = parts + lax.ppermute(parts, axis, [(i, i ^ bit) for i in range(size)])
        steps.append(parts)
    totals = parts[0]
    outgoing = grad_part(
        place, far_inputs, far_pieces, grads, IMAGES, IMAGES, BF16, "grad_far_sent", [steps[0]]
    )
    incoming = swap_cores(outgoing)
    kept = grad_part(
        place, far_inputs, far_pieces, grads, 0, IMAGES, F32, "grad_far_kept", [steps[1], outgoing]
    )

    cov_sum, inv_sum, var_sum = totals[0], totals[1], totals[2]
    total_feats = 8 * FEATS
    total_loss = (
        25.0 * inv_sum / (BATCH * total_feats)
        + 25.0 * var_sum / total_feats
        + cov_sum / total_feats
    )
    gradient = base + BATCH / (16.0 * (BATCH - 1)) * (kept + incoming.astype(F32))
    return (gradient, total_loss)


def solution(mesh):
    in_specs = (P("col", "row"), P("col", "row"))
    out_specs = (P("col", "row"), P())
    return jax.shard_map(
        per_device, mesh=mesh, in_specs=in_specs, out_specs=out_specs, check_vma=False
    )
```

```python
import functools

import jax
import jax.numpy as jnp
from jax import lax
from jax.experimental import pallas as pl
from jax.experimental.pallas import tpu as pltpu
from jax.sharding import PartitionSpec as P

F32 = jnp.float32
BF16 = jnp.bfloat16
IMAGES, FEATS, CHIPS = 768, 512, 8
BATCH = IMAGES * 16
CHIP_IMAGES = 2 * IMAGES
HALF = FEATS // 2
STAT_ROWS = 16
GRAD_SCALE = BATCH / (16.0 * (BATCH - 1))

QUARTER = FEATS // 4
VMEM = pl.BlockSpec(memory_space=pltpu.VMEM)
SMEM = pl.BlockSpec(memory_space=pltpu.SMEM)
ANY = pl.BlockSpec(memory_space=pl.ANY)


def shift_row(block, dx, dz):
    pairs = [(2 * x + z, 2 * ((x + dx) % 4) + (z + dz) % 2) for x in range(4) for z in range(2)]
    return lax.ppermute(block, "row", pairs)


def flip(block, z_lo, core):
    pairs = []
    for row in range(8):
        for col in range(16):
            pairs.append((16 * row + col, 16 * (row ^ z_lo) + (col ^ core)))
    return lax.ppermute(block, ("row", "col"), pairs)


def swap_cores(block):
    return lax.ppermute(block, "col", [(i, i ^ 1) for i in range(16)])


def shift_y(block, dy):
    pairs = [
        (8 * z + 2 * y + core, 8 * z + 2 * ((y + dy) % 4) + core)
        for z in range(2) for y in range(4) for core in range(2)
    ]
    return lax.ppermute(block, "col", pairs)


def swap_z_hi(block):
    return lax.ppermute(block, "col", [(i, i ^ 8) for i in range(16)])


def call(body, outs, ins, scratch, name, after=(), flops=0):
    count, waits = len(ins), len(after)

    def kernel(*refs):
        body(*refs[:count], *refs[count + waits:])

    return pl.pallas_call(
        kernel,
        out_shape=tuple(outs),
        in_specs=[SMEM if a.dtype == jnp.int32 else VMEM for a in ins] + [ANY] * waits,
        out_specs=tuple(VMEM for _ in outs),
        scratch_shapes=scratch,
        compiler_params=pltpu.CompilerParams(vmem_limit_bytes=16 * 2**20),
        cost_estimate=pl.CostEstimate(flops=flops, bytes_accessed=0, transcendentals=0),
        name=name,
    )(*ins, *after)


def shape(dims, dtype):
    return jax.ShapeDtypeStruct(dims, dtype)


def layout(chunks):
    places, column, at = [], 0, 0
    while at < len(chunks):
        rows, width = chunks[at].shape
        count = CHIP_IMAGES // rows
        for part in range(count):
            places.append((at + part, part * rows, column))
        column += width
        at += count
    return places, column


def split3(value):
    high = value.astype(BF16).astype(F32)
    middle = (value - high).astype(BF16).astype(F32)
    return [high, middle, value - high - middle]


def column_sum(ref):
    ones = jnp.ones((8, ref.shape[0]), BF16)
    return jnp.dot(ones, ref[...], preferred_element_type=F32)[0:1]


def center_into(target, first, column, ref, mean):
    width = ref.shape[1]
    step = 128

    def body(i, carry):
        at = pl.multiple_of(i * step, step)
        block = ref[pl.ds(at, step), :].astype(F32) - mean
        target[pl.ds(first + at, step), column:column + width] = block.astype(BF16)
        return carry

    lax.fori_loop(0, ref.shape[0] // step, body, 0)


def fill_columns(places, refs, columns, stats):
    means = {}
    for at, _, column in places:
        means[column] = means.get(column, 0.0) + column_sum(refs[at])
    for column, total in means.items():
        mean = total / CHIP_IMAGES
        stats[0:1, column:column + mean.shape[1]] = mean
        means[column] = mean
    for at, first, column in places:
        center_into(columns, first, column, refs[at], means[column])


def center_rows(target, first, ref, mean):
    step = 128

    def body(i, total):
        at = pl.multiple_of(i * step, step)
        block = ref[pl.ds(at, step), :].astype(F32) - mean
        target[pl.ds(first + at, step), :] = block.astype(BF16)
        return total + jnp.sum((block * block).reshape(step // 8, 8, FEATS), axis=0)

    total = lax.fori_loop(0, ref.shape[0] // step, body, jnp.zeros((8, FEATS), F32))
    return jnp.sum(total, axis=0, keepdims=True)


def padded(lines, width):
    pad = width - lines[0].shape[1]
    return [jnp.concatenate([line, jnp.zeros((line.shape[0], pad), F32)], axis=1) for line in lines]


def filled(lines, width):
    count = sum(line.shape[0] for line in lines)
    lines = lines + [jnp.zeros((-count % STAT_ROWS, width), F32)]
    return jnp.concatenate([line for line in lines if line.shape[0]], axis=0)


def rows_kernel(own, sibling, teacher, rows_t, row_stats, parts, rows):
    row_mean = (column_sum(own) + column_sum(sibling)) / CHIP_IMAGES
    squares = center_rows(rows, 0, own, row_mean) + center_rows(rows, IMAGES, sibling, row_mean)
    for at in range(0, FEATS, 128):
        rows_t[at:at + 128, :] = rows[:, at:at + 128].T
    row_stats[...] = jnp.concatenate([row_mean, squares, jnp.zeros((6, FEATS), F32)], axis=0)

    def body(i, total):
        at = pl.ds(pl.multiple_of(i * 128, 128), 128)
        diff = own[at, :].astype(F32) - teacher[at, :].astype(F32)
        return total + jnp.sum((diff * diff).reshape(16, 8, FEATS), axis=0)

    total = lax.fori_loop(0, IMAGES // 128, body, jnp.zeros((8, FEATS), F32))
    lanes = lax.broadcasted_iota(jnp.int32, parts.shape, 1)
    parts[...] = jnp.where(lanes == 1, jnp.sum(total, keepdims=True), 0.0)


def center_own(own, sibling, teacher, after):
    return call(
        rows_kernel,
        [shape((FEATS, CHIP_IMAGES), BF16), shape((8, FEATS), F32), shape((8, 128), F32)],
        [own, sibling, teacher],
        [pltpu.VMEM((CHIP_IMAGES, FEATS), BF16)],
        "center_own",
        after,
    )


def join_kernel(first, second, out):
    out[0:IMAGES, :] = first[...]
    out[IMAGES:CHIP_IMAGES, :] = second[...]


def join(first, second, after=()):
    return call(
        join_kernel, [shape((CHIP_IMAGES, HALF), BF16)], [first, second], [], "join", after
    )[0]


def base_kernel(student, teacher, row_stats, out):
    mean, spread = row_stats[0:1, :], row_stats[1:2, :]
    scale = jnp.where(spread < 1.0, 25.0 * BATCH / 64.0 / (spread * (BATCH - 1)), 0.0)

    def body(i, carry):
        at = pl.ds(pl.multiple_of(i * 64, 64), 64)
        value = student[at, :].astype(F32)
        diff = value - teacher[at, :].astype(F32)
        out[at, :] = (25.0 / 32.0) * diff - scale * (value - mean)
        return carry

    lax.fori_loop(0, IMAGES // 64, body, 0)


def base_part(student, teacher, row_stats, after):
    ins = [student, teacher, row_stats]
    return call(base_kernel, [shape((IMAGES, FEATS), F32)], ins, [], "base", after)[0]


def partial_kernel(places, width, count, with_rows, *refs):
    place, rows_t, row_stats = refs[:3]
    chunks = refs[3:3 + count]
    pieces = refs[3 + count:7 + count]
    columns, stats, sums = refs[7 + count:]
    fill_columns(places, chunks, columns, stats)
    for at in range(0, width, 256):
        sums[:, at:at + 256] = jnp.dot(
            rows_t[...], columns[:, at:at + 256], preferred_element_type=F32
        )
    lines = split3(stats[0:1, :])
    if with_rows:
        lines += padded(split3(row_stats[0:1, :]) + split3(row_stats[1:2, :]), width)
    block = filled(lines, width)
    for d in range(4):
        first = pl.multiple_of((place[2] + d) % 4 * QUARTER, QUARTER)
        pieces[d][0:QUARTER, :] = sums[pl.ds(first, QUARTER), :].astype(pieces[d].dtype)
        pieces[d][QUARTER:QUARTER + STAT_ROWS, :] = block.astype(pieces[d].dtype)


def partial_sums(place, rows_t, row_stats, chunks, with_rows, name, after=()):
    places, width = layout(chunks)
    rows = QUARTER + STAT_ROWS
    *pieces, columns, stats = call(
        functools.partial(partial_kernel, places, width, len(chunks), with_rows),
        [shape((rows, width), F32)]
        + [shape((rows, width), BF16)] * 3
        + [shape((CHIP_IMAGES, width), BF16), shape((8, width), F32)],
        [place, rows_t, row_stats] + chunks,
        [pltpu.VMEM((FEATS, width), F32)],
        name,
        after,
        flops=40 * CHIP_IMAGES * FEATS * width,
    )
    return pieces, columns, stats


def spread_out(local):
    mean = jnp.sum(local, axis=0, keepdims=True) / CHIPS
    return local - mean, mean


def mean_term(row_offsets, col_offsets):
    return CHIP_IMAGES * lax.dot_general(
        row_offsets,
        col_offsets,
        (((0,), (0,)), ((), ())),
        precision=lax.Precision.HIGHEST,
        preferred_element_type=F32,
    )


def three(stats, first):
    return stats[first:first + 1] + stats[first + 1:first + 2] + stats[first + 2:first + 3]


def combine_y_kernel(
    with_rows, place, parts, own, one, two, three_on, plane, message, local, *row_local
):
    width = own.shape[1]
    columns = jnp.zeros((4, width), F32)
    rows = jnp.zeros((4, FEATS), F32)
    squares = jnp.zeros((1, FEATS), F32)
    total = own[0:QUARTER, :]
    for d, piece in enumerate((own, one, two, three_on)):
        if d:
            total = total + piece[0:QUARTER, :].astype(F32)
        at = (place[2] + 4 - d) % 4
        stats = piece[QUARTER:QUARTER + STAT_ROWS, :].astype(F32)
        here = lax.broadcasted_iota(jnp.int32, columns.shape, 0) == at
        columns = jnp.where(here, three(stats, 0), columns)
        if with_rows:
            here = lax.broadcasted_iota(jnp.int32, rows.shape, 0) == at
            rows = jnp.where(here, three(stats[:, 0:FEATS], 3), rows)
            squares = squares + three(stats[:, 0:FEATS], 6)

    def rounded(value):
        high, middle, low = split3(value)
        low = low.astype(BF16).astype(F32)
        return [high, middle, low], high + middle + low

    plane[...] = total.astype(BF16)
    message[0:QUARTER, :] = total.astype(BF16)
    lines, local[0:4, :] = rounded(columns)
    if with_rows:
        row_lines, row_local[0][0:4, :] = rounded(rows)
        square_lines, row_local[0][4:5, :] = rounded(squares)
        part_lines, _ = rounded(parts[0:1, :])
        lines = lines + padded(row_lines + square_lines, width) + padded(part_lines, width)
    block = filled(lines, width)
    message[QUARTER:QUARTER + block.shape[0], :] = block.astype(BF16)


def combine_y(place, parts, pieces, with_rows, name, after=()):
    width = pieces[0].shape[1]
    rows = QUARTER + (2 if with_rows else 1) * STAT_ROWS
    outs = [shape((QUARTER, width), BF16), shape((rows, width), BF16), shape((8, width), F32)]
    outs += [shape((8, FEATS), F32)] if with_rows else []
    return call(
        functools.partial(combine_y_kernel, with_rows), outs, [place, parts] + pieces, [], name, after
    )


def all_chips(place, mine, theirs):
    low = place[3] == 0
    return jnp.concatenate([jnp.where(low, mine, theirs), jnp.where(low, theirs, mine)], axis=0)


def combine_z_kernel(
    with_rows, place, plane, local, rows, received, parts, masked, part, means, *more
):
    stats = received[QUARTER:, :].astype(F32)
    theirs = stats[0:4] + stats[4:8] + stats[8:12]
    col_off, col_mean = spread_out(all_chips(place, local[0:4, :], theirs))
    means[...] = jnp.broadcast_to(col_mean, means.shape)
    row_offsets = rows
    if with_rows:
        row_offsets, row_stats = more
        other_parts = three(stats[:, 0:128], 27)
        stats = stats[:, 0:FEATS]
        theirs = stats[12:16] + stats[16:20] + stats[20:24]
        row_off, row_mean = spread_out(all_chips(place, rows[0:4, :], theirs))
        squares = rows[4:5, :] + three(stats, 24)
        squares = squares + CHIP_IMAGES * jnp.sum(row_off * row_off, axis=0, keepdims=True)
        variance = squares / (BATCH - 1)
        row_offsets[...] = row_off
        spread = jnp.sqrt(variance + 0.0001)
        row_stats[...] = jnp.concatenate([row_mean, spread, jnp.zeros((6, FEATS), F32)], axis=0)
    block = pl.multiple_of(place[2] * QUARTER, QUARTER)
    term = mean_term(row_offsets[:, pl.ds(block, QUARTER)], col_off)
    covar = plane[...].astype(F32) + received[0:QUARTER, :].astype(F32)
    covar = (covar + term) / (BATCH - 1)
    if with_rows:
        row_ids = place[2] * QUARTER + lax.broadcasted_iota(jnp.int32, covar.shape, 0)
        col_ids = lax.broadcasted_iota(jnp.int32, covar.shape, 1)
        on_diagonal = (col_ids < HALF) & (row_ids == col_ids + place[1] * HALF)
        covar = jnp.where(on_diagonal, F32(0.0), covar)
    lanes = lax.broadcasted_iota(jnp.int32, part.shape, 1)
    found = jnp.where(lanes == 0, jnp.sum(covar * covar, keepdims=True), 0.0)
    if with_rows:
        var_part = jnp.sum(jnp.maximum(0.0, 1.0 - spread), keepdims=True) / 8
        found = found + jnp.where(lanes == 2, var_part, 0.0) + other_parts
    part[...] = parts[...] + found
    masked[0:QUARTER, :] = covar.astype(BF16)
    if not with_rows:
        block = filled(padded(split3(part[0:1, :]), covar.shape[1]), covar.shape[1])
        masked[QUARTER:QUARTER + STAT_ROWS, :] = block.astype(BF16)


def combine_z(place, plane, local, rows, received, parts, with_rows, name, after=()):
    width = plane.shape[1]
    count = QUARTER + (0 if with_rows else STAT_ROWS)
    outs = [shape((count, width), BF16), shape((8, 128), F32), shape((8, width), F32)]
    outs += [shape((8, FEATS), F32)] * 2 if with_rows else []
    ins = [place, plane, local, rows, received, parts]
    return call(functools.partial(combine_z_kernel, with_rows), outs, ins, [], name, after)


def parts_kernel(place, own, one, two, three_on, out):
    lines = jnp.zeros((4, 128), F32)
    for d, piece in enumerate((own, one, two, three_on)):
        here = lax.broadcasted_iota(jnp.int32, lines.shape, 0) == (place[2] + 4 - d) % 4
        lines = jnp.where(here, three(piece[QUARTER:, 0:128].astype(F32), 0), lines)
    out[...] = jnp.broadcast_to(jnp.sum(lines, axis=0, keepdims=True), out.shape)


def sum_parts(place, pieces, after):
    return call(
        parts_kernel, [shape((8, 128), F32)], [place] + pieces, [], "sum_parts", after
    )[0]


def x_kernel(place, own, one, two, three_on, out):
    total = jnp.zeros((8, 128), F32)
    for x in range(4):
        block = own[...]
        for d, other in ((1, one), (2, two), (3, three_on)):
            block = jnp.where((place[4] + 4 - d) % 4 == x, other[...], block)
        total = total + block
    out[...] = total


def loss_kernel(own, other_z, other_core, other_both, out):
    total = (own[...] + other_z[...]) + (other_core[...] + other_both[...])
    loss = total[:, 0:1] + 25.0 * (total[:, 1:2] / BATCH + total[:, 2:3])
    out[...] = jnp.broadcast_to(loss / (8 * FEATS), out.shape)


def sum_x(place, blocks):
    return call(x_kernel, [shape((8, 128), F32)], [place] + blocks, [], "sum_x")[0]


def loss_of(blocks):
    return call(loss_kernel, [shape((8, 128), F32)], blocks, [], "loss")[0]


def shift_term(stats, means, masked):
    lines = filled(split3(stats[0:1, :] - means[0:1, :]), stats.shape[1]).astype(BF16)
    rows = lax.dot_general(
        lines, masked[...], (((1,), (1,)), ((), ())), preferred_element_type=F32
    )
    return rows[0:1] + rows[1:2] + rows[2:3]


def times_masked(columns, at, masked):
    return lax.dot_general(
        columns[at:at + 256, :], masked[...], (((1,), (1,)), ((), ())), preferred_element_type=F32
    )


def grad_kernel(
    first, rows, add, with_base, place, columns, stats, means, own, one, two, three_on, *rest
):
    out, masked = rest[-2:]
    for d, piece in enumerate((own, one, two, three_on)):
        row = pl.multiple_of((place[2] + 4 - d) % 4 * QUARTER, QUARTER)
        masked[pl.ds(row, QUARTER), :] = piece[0:QUARTER, :]
    shift = shift_term(stats, means, masked)
    for at in range(first, first + rows, 256):
        product = times_masked(columns, at, masked) + shift
        if add:
            product = product + rest[0][at:at + 256, :]
        if with_base:
            product = GRAD_SCALE * product + rest[1][at:at + 256, :]
        out[at - first:at - first + 256, :] = product.astype(out.dtype)


def grad_part(place, inputs, pieces, previous, first, rows, dtype, name, after=(), base=None):
    columns, stats, means = inputs
    ins = [place, columns, stats, means] + pieces
    ins += [a for a in (previous, base) if a is not None]
    return call(
        functools.partial(
            grad_kernel, first, rows, previous is not None, base is not None
        ),
        [shape((rows, FEATS), dtype)],
        ins,
        [pltpu.VMEM((FEATS, columns.shape[1]), BF16)],
        name,
        after,
    )[0]


def per_device(student, teacher):
    row_index = lax.axis_index("row")
    col_index = lax.axis_index("col")
    core = col_index % 2
    chip = col_index // 2
    place = jnp.stack([chip, core, chip % 4, chip // 4, row_index // 2]).astype(jnp.int32)

    sibling = swap_cores(student)
    own_a = lax.dynamic_slice_in_dim(student, core * HALF, HALF, 1)
    x_lo_a = shift_row(own_a, 1, 0)
    x_hi_a = shift_row(own_a, -1, 0)
    own_b = lax.dynamic_slice_in_dim(sibling, core * HALF, HALF, 1)
    x_lo_b = shift_row(own_b, 1, 0)
    x_hi_b = shift_row(own_b, -1, 0)
    z_own_a = shift_row(own_a, 0, 1)
    z_own_b = shift_row(own_b, 0, 1)
    rows_t, own_stats, parts = center_own(student, sibling, teacher, [x_lo_a])
    x_lo_a, x_lo_b = lax.optimization_barrier((x_lo_a, x_lo_b))
    x_far_a = shift_row(x_lo_a, 1, 0)
    x_far_b = shift_row(x_hi_b, -1, 0)
    near = [own_a, own_b, x_lo_a, x_lo_b, x_hi_a, x_hi_b, z_own_a, z_own_b]

    near_sums, near_columns, near_stats = partial_sums(
        place, rows_t, own_stats, near, True, "partial_near"
    )
    z_own = join(z_own_a, z_own_b, [near_stats])
    z_lo = shift_row(z_own, 1, 0)
    z_hi = shift_row(z_own, -1, 0)
    x_far = join(x_far_a, x_far_b, [z_own])
    z_far = shift_row(x_far, 0, 1)
    far = [x_far, z_lo, z_hi, z_far]
    near_sums[1:] = [shift_y(near_sums[d], d) for d in (1, 2, 3)]
    far_sums, far_columns, far_stats = partial_sums(
        place, rows_t, own_stats, far, False, "partial_far"
    )
    far_sums[1:] = [shift_y(far_sums[d], d) for d in (1, 2, 3)]

    plane, message, local, row_local = combine_y(
        place, parts, near_sums, True, "combine_y_near", [far_sums[0]]
    )
    far_plane, far_message, far_local = combine_y(
        place, parts, far_sums, False, "combine_y_far", [plane]
    )
    near_masked, parts, near_means, row_offsets, row_stats = combine_z(
        place, plane, local, row_local, swap_z_hi(message), parts, True,
        "combine_z_near",
        [far_plane],
    )
    near_pieces = [near_masked] + [shift_y(near_masked, d) for d in (1, 2, 3)]
    far_masked, _, far_means = combine_z(
        place, far_plane, far_local, row_offsets, swap_z_hi(far_message), parts, False,
        "combine_z_far", near_pieces[1:],
    )
    far_pieces = [far_masked] + [shift_y(far_masked, d) for d in (1, 2, 3)]

    base = base_part(student, teacher, row_stats, [far_masked])
    near_inputs = (near_columns, near_stats, near_means)
    far_inputs = (far_columns, far_stats, far_means)
    grads = grad_part(
        place, near_inputs, near_pieces, None, 0, CHIP_IMAGES, F32, "grad_near", [base]
    )
    parts = sum_parts(place, far_pieces, [grads])
    outgoing = grad_part(
        place, far_inputs, far_pieces, grads, IMAGES, IMAGES, BF16, "grad_far_sent", [parts]
    )
    incoming = swap_cores(outgoing)
    row_parts = sum_x(place, [parts] + [shift_row(parts, dx, 0) for dx in (1, 2, 3)])
    kept = grad_part(
        place, far_inputs, far_pieces, grads, 0, IMAGES, F32, "grad_far_kept",
        [row_parts, outgoing], base,
    )
    total_loss = loss_of([row_parts] + [flip(row_parts, *way) for way in ((1, 0), (0, 1), (1, 1))])
    return (kept + GRAD_SCALE * incoming.astype(F32), total_loss[0, 0])


def solution(mesh):
    in_specs = (P("col", "row"), P("col", "row"))
    out_specs = (P("col", "row"), P())
    return jax.shard_map(
        per_device, mesh=mesh, in_specs=in_specs, out_specs=out_specs, check_vma=False
    )
```

```python
import functools

import jax
import jax.numpy as jnp
from jax import lax
from jax.experimental import pallas as pl
from jax.experimental.pallas import tpu as pltpu
from jax.sharding import PartitionSpec as P

F32 = jnp.float32
BF16 = jnp.bfloat16
IMAGES, FEATS, CHIPS = 768, 512, 8
BATCH = IMAGES * 16
CHIP_IMAGES = 2 * IMAGES
HALF = FEATS // 2
STAT_ROWS = 16
GRAD_SCALE = BATCH / (16.0 * (BATCH - 1))

QUARTER = FEATS // 4
VMEM = pl.BlockSpec(memory_space=pltpu.VMEM)
SMEM = pl.BlockSpec(memory_space=pltpu.SMEM)
ANY = pl.BlockSpec(memory_space=pl.ANY)


def shift_row(block, dx, dz):
    pairs = [(2 * x + z, 2 * ((x + dx) % 4) + (z + dz) % 2) for x in range(4) for z in range(2)]
    return lax.ppermute(block, "row", pairs)


def flip(block, z_lo, core):
    pairs = []
    for row in range(8):
        for col in range(16):
            pairs.append((16 * row + col, 16 * (row ^ z_lo) + (col ^ core)))
    return lax.ppermute(block, ("row", "col"), pairs)


def swap_cores(block):
    return lax.ppermute(block, "col", [(i, i ^ 1) for i in range(16)])


def shift_y(block, dy):
    pairs = [
        (8 * z + 2 * y + core, 8 * z + 2 * ((y + dy) % 4) + core)
        for z in range(2) for y in range(4) for core in range(2)
    ]
    return lax.ppermute(block, "col", pairs)


def sent_round(block):
    two, one, three_on = [shift_y(block, d) for d in (2, 1, 3)]
    return [block, one, two, three_on]


def swap_z_hi(block):
    return lax.ppermute(block, "col", [(i, i ^ 8) for i in range(16)])


def call(body, outs, ins, scratch, name, after=(), flops=0):
    count, waits = len(ins), len(after)

    def kernel(*refs):
        body(*refs[:count], *refs[count + waits:])

    return pl.pallas_call(
        kernel,
        out_shape=tuple(outs),
        in_specs=[SMEM if a.dtype == jnp.int32 else VMEM for a in ins] + [ANY] * waits,
        out_specs=tuple(VMEM for _ in outs),
        scratch_shapes=scratch,
        compiler_params=pltpu.CompilerParams(vmem_limit_bytes=16 * 2**20),
        cost_estimate=pl.CostEstimate(flops=flops, bytes_accessed=0, transcendentals=0),
        name=name,
    )(*ins, *after)


def shape(dims, dtype):
    return jax.ShapeDtypeStruct(dims, dtype)


def layout(chunks):
    places, column, at = [], 0, 0
    while at < len(chunks):
        rows, width = chunks[at].shape
        count = CHIP_IMAGES // rows
        for part in range(count):
            places.append((at + part, part * rows, column))
        column += width
        at += count
    return places, column


def split3(value):
    high = value.astype(BF16).astype(F32)
    middle = (value - high).astype(BF16).astype(F32)
    return [high, middle, value - high - middle]


def column_sum(ref):
    ones = jnp.ones((8, ref.shape[0]), BF16)
    return jnp.dot(ones, ref[...], preferred_element_type=F32)[0:1]


def center_into(target, first, column, ref, mean):
    width = ref.shape[1]
    step = 128

    def body(i, carry):
        at = pl.multiple_of(i * step, step)
        block = ref[pl.ds(at, step), :].astype(F32) - mean
        target[pl.ds(first + at, step), column:column + width] = block.astype(BF16)
        return carry

    lax.fori_loop(0, ref.shape[0] // step, body, 0)


def fill_columns(places, refs, columns, stats):
    means = {}
    for at, _, column in places:
        means[column] = means.get(column, 0.0) + column_sum(refs[at])
    for column, total in means.items():
        mean = total / CHIP_IMAGES
        stats[0:1, column:column + mean.shape[1]] = mean
        means[column] = mean
    for at, first, column in places:
        center_into(columns, first, column, refs[at], means[column])


def center_rows(target, first, ref, mean):
    step = 128

    def body(i, total):
        at = pl.multiple_of(i * step, step)
        block = ref[pl.ds(at, step), :].astype(F32) - mean
        target[pl.ds(first + at, step), :] = block.astype(BF16)
        return total + jnp.sum((block * block).reshape(step // 8, 8, FEATS), axis=0)

    total = lax.fori_loop(0, ref.shape[0] // step, body, jnp.zeros((8, FEATS), F32))
    return jnp.sum(total, axis=0, keepdims=True)


def padded(lines, width):
    pad = width - lines[0].shape[1]
    return [jnp.concatenate([line, jnp.zeros((line.shape[0], pad), F32)], axis=1) for line in lines]


def filled(lines, width):
    count = sum(line.shape[0] for line in lines)
    lines = lines + [jnp.zeros((-count % STAT_ROWS, width), F32)]
    return jnp.concatenate([line for line in lines if line.shape[0]], axis=0)


def rows_kernel(own, sibling, teacher, rows_t, row_stats, parts, rows):
    row_mean = (column_sum(own) + column_sum(sibling)) / CHIP_IMAGES
    squares = center_rows(rows, 0, own, row_mean) + center_rows(rows, IMAGES, sibling, row_mean)
    for at in range(0, FEATS, 128):
        rows_t[at:at + 128, :] = rows[:, at:at + 128].T
    row_stats[...] = jnp.concatenate([row_mean, squares, jnp.zeros((6, FEATS), F32)], axis=0)

    def body(i, total):
        at = pl.ds(pl.multiple_of(i * 128, 128), 128)
        diff = own[at, :].astype(F32) - teacher[at, :].astype(F32)
        return total + jnp.sum((diff * diff).reshape(16, 8, FEATS), axis=0)

    total = lax.fori_loop(0, IMAGES // 128, body, jnp.zeros((8, FEATS), F32))
    lanes = lax.broadcasted_iota(jnp.int32, parts.shape, 1)
    parts[...] = jnp.where(lanes == 1, jnp.sum(total, keepdims=True), 0.0)


def center_own(own, sibling, teacher, after):
    return call(
        rows_kernel,
        [shape((FEATS, CHIP_IMAGES), BF16), shape((8, FEATS), F32), shape((8, 128), F32)],
        [own, sibling, teacher],
        [pltpu.VMEM((CHIP_IMAGES, FEATS), BF16)],
        "center_own",
        after,
    )


def join_kernel(first, second, out):
    out[0:IMAGES, :] = first[...]
    out[IMAGES:CHIP_IMAGES, :] = second[...]


def join(first, second, after=()):
    return call(
        join_kernel, [shape((CHIP_IMAGES, HALF), BF16)], [first, second], [], "join", after
    )[0]


def base_kernel(student, teacher, row_stats, out):
    mean, spread = row_stats[0:1, :], row_stats[1:2, :]
    scale = jnp.where(spread < 1.0, 25.0 * BATCH / 64.0 / (spread * (BATCH - 1)), 0.0)

    def body(i, carry):
        at = pl.ds(pl.multiple_of(i * 64, 64), 64)
        value = student[at, :].astype(F32)
        diff = value - teacher[at, :].astype(F32)
        out[at, :] = (25.0 / 32.0) * diff - scale * (value - mean)
        return carry

    lax.fori_loop(0, IMAGES // 64, body, 0)


def base_part(student, teacher, row_stats, after):
    ins = [student, teacher, row_stats]
    return call(base_kernel, [shape((IMAGES, FEATS), F32)], ins, [], "base", after)[0]


def partial_kernel(places, width, count, with_rows, *refs):
    place, rows_t, row_stats = refs[:3]
    chunks = refs[3:3 + count]
    pieces = refs[3 + count:7 + count]
    columns, stats, sums = refs[7 + count:]
    fill_columns(places, chunks, columns, stats)
    for at in range(0, width, 256):
        sums[:, at:at + 256] = jnp.dot(
            rows_t[...], columns[:, at:at + 256], preferred_element_type=F32
        )
    lines = split3(stats[0:1, :])
    if with_rows:
        lines += padded(split3(row_stats[0:1, :]) + split3(row_stats[1:2, :]), width)
    block = filled(lines, width)
    for d in range(4):
        first = pl.multiple_of((place[2] + d) % 4 * QUARTER, QUARTER)
        pieces[d][0:QUARTER, :] = sums[pl.ds(first, QUARTER), :].astype(pieces[d].dtype)
        pieces[d][QUARTER:QUARTER + STAT_ROWS, :] = block.astype(pieces[d].dtype)


def partial_sums(place, rows_t, row_stats, chunks, with_rows, name, after=()):
    places, width = layout(chunks)
    rows = QUARTER + STAT_ROWS
    *pieces, columns, stats = call(
        functools.partial(partial_kernel, places, width, len(chunks), with_rows),
        [shape((rows, width), F32)]
        + [shape((rows, width), BF16)] * 3
        + [shape((CHIP_IMAGES, width), BF16), shape((8, width), F32)],
        [place, rows_t, row_stats] + chunks,
        [pltpu.VMEM((FEATS, width), F32)],
        name,
        after,
        flops=40 * CHIP_IMAGES * FEATS * width,
    )
    return pieces, columns, stats


def spread_out(local):
    mean = jnp.sum(local, axis=0, keepdims=True) / CHIPS
    return local - mean, mean


def mean_term(row_offsets, col_offsets):
    return CHIP_IMAGES * lax.dot_general(
        row_offsets,
        col_offsets,
        (((0,), (0,)), ((), ())),
        precision=lax.Precision.HIGHEST,
        preferred_element_type=F32,
    )


def three(stats, first):
    return stats[first:first + 1] + stats[first + 1:first + 2] + stats[first + 2:first + 3]


def combine_y_kernel(
    with_rows, place, parts, own, one, two, three_on, plane, message, local, *row_local
):
    width = own.shape[1]
    columns = jnp.zeros((4, width), F32)
    rows = jnp.zeros((4, FEATS), F32)
    squares = jnp.zeros((1, FEATS), F32)
    total = own[0:QUARTER, :]
    for d, piece in enumerate((own, one, two, three_on)):
        if d:
            total = total + piece[0:QUARTER, :].astype(F32)
        at = (place[2] + 4 - d) % 4
        stats = piece[QUARTER:QUARTER + STAT_ROWS, :].astype(F32)
        here = lax.broadcasted_iota(jnp.int32, columns.shape, 0) == at
        columns = jnp.where(here, three(stats, 0), columns)
        if with_rows:
            here = lax.broadcasted_iota(jnp.int32, rows.shape, 0) == at
            rows = jnp.where(here, three(stats[:, 0:FEATS], 3), rows)
            squares = squares + three(stats[:, 0:FEATS], 6)

    def rounded(value):
        high, middle, low = split3(value)
        low = low.astype(BF16).astype(F32)
        return [high, middle, low], high + middle + low

    plane[...] = total.astype(BF16)
    message[0:QUARTER, :] = total.astype(BF16)
    lines, local[0:4, :] = rounded(columns)
    if with_rows:
        row_lines, row_local[0][0:4, :] = rounded(rows)
        square_lines, row_local[0][4:5, :] = rounded(squares)
        part_lines, _ = rounded(parts[0:1, :])
        lines = lines + padded(row_lines + square_lines, width) + padded(part_lines, width)
    block = filled(lines, width)
    message[QUARTER:QUARTER + block.shape[0], :] = block.astype(BF16)


def combine_y(place, parts, pieces, with_rows, name, after=()):
    width = pieces[0].shape[1]
    rows = QUARTER + (2 if with_rows else 1) * STAT_ROWS
    outs = [shape((QUARTER, width), BF16), shape((rows, width), BF16), shape((8, width), F32)]
    outs += [shape((8, FEATS), F32)] if with_rows else []
    return call(
        functools.partial(combine_y_kernel, with_rows), outs, [place, parts] + pieces, [], name, after
    )


def all_chips(place, mine, theirs):
    low = place[3] == 0
    return jnp.concatenate([jnp.where(low, mine, theirs), jnp.where(low, theirs, mine)], axis=0)


def combine_z_kernel(
    with_rows, place, plane, local, rows, received, parts, masked, part, means, *more
):
    stats = received[QUARTER:, :].astype(F32)
    theirs = stats[0:4] + stats[4:8] + stats[8:12]
    col_off, col_mean = spread_out(all_chips(place, local[0:4, :], theirs))
    means[...] = jnp.broadcast_to(col_mean, means.shape)
    row_offsets = rows
    if with_rows:
        row_offsets, row_stats = more
        other_parts = three(stats[:, 0:128], 27)
        stats = stats[:, 0:FEATS]
        theirs = stats[12:16] + stats[16:20] + stats[20:24]
        row_off, row_mean = spread_out(all_chips(place, rows[0:4, :], theirs))
        squares = rows[4:5, :] + three(stats, 24)
        squares = squares + CHIP_IMAGES * jnp.sum(row_off * row_off, axis=0, keepdims=True)
        variance = squares / (BATCH - 1)
        row_offsets[...] = row_off
        spread = jnp.sqrt(variance + 0.0001)
        row_stats[...] = jnp.concatenate([row_mean, spread, jnp.zeros((6, FEATS), F32)], axis=0)
    block = pl.multiple_of(place[2] * QUARTER, QUARTER)
    term = mean_term(row_offsets[:, pl.ds(block, QUARTER)], col_off)
    covar = plane[...].astype(F32) + received[0:QUARTER, :].astype(F32)
    covar = (covar + term) / (BATCH - 1)
    if with_rows:
        row_ids = place[2] * QUARTER + lax.broadcasted_iota(jnp.int32, covar.shape, 0)
        col_ids = lax.broadcasted_iota(jnp.int32, covar.shape, 1)
        on_diagonal = (col_ids < HALF) & (row_ids == col_ids + place[1] * HALF)
        covar = jnp.where(on_diagonal, F32(0.0), covar)
    lanes = lax.broadcasted_iota(jnp.int32, part.shape, 1)
    found = jnp.where(lanes == 0, jnp.sum(covar * covar, keepdims=True), 0.0)
    if with_rows:
        var_part = jnp.sum(jnp.maximum(0.0, 1.0 - spread), keepdims=True) / 8
        found = found + jnp.where(lanes == 2, var_part, 0.0) + other_parts
    part[...] = parts[...] + found
    masked[0:QUARTER, :] = covar.astype(BF16)


def combine_z(place, plane, local, rows, received, parts, with_rows, name, after=()):
    width = plane.shape[1]
    outs = [shape((QUARTER, width), BF16), shape((8, 128), F32), shape((8, width), F32)]
    outs += [shape((8, FEATS), F32)] * 2 if with_rows else []
    ins = [place, plane, local, rows, received, parts]
    return call(functools.partial(combine_z_kernel, with_rows), outs, ins, [], name, after)


def add_kernel(one, two, out):
    out[...] = one[...] + two[...]


def add_four_kernel(one, two, three_on, four, out):
    out[...] = (one[...] + two[...]) + (three_on[...] + four[...])


def loss_kernel(one, two, three_on, four, out):
    total = (one[...] + two[...]) + (three_on[...] + four[...])
    loss = total[:, 0:1] + 25.0 * (total[:, 1:2] / BATCH + total[:, 2:3])
    out[...] = jnp.broadcast_to(loss / (8 * FEATS), out.shape)


def flip(parts, row_bits, col_bits):
    if not row_bits:
        return lax.ppermute(parts, "col", [(i, i ^ col_bits) for i in range(16)])
    if not col_bits:
        return lax.ppermute(parts, "row", [(i, i ^ row_bits) for i in range(8)])
    pairs = [
        (16 * row + col, 16 * (row ^ row_bits) + (col ^ col_bits))
        for row in range(8) for col in range(16)
    ]
    return lax.ppermute(parts, ("row", "col"), pairs)


def pair_sum(parts, row_bits, col_bits, after=()):
    ins = [parts, flip(parts, row_bits, col_bits)]
    return call(add_kernel, [shape((8, 128), F32)], ins, [], "pair_sum", after)[0]


def four_sum(parts, first, second, body, name, after=()):
    both = (first[0] | second[0], first[1] | second[1])
    ins = [parts] + [flip(parts, *bits) for bits in (first, second, both)]
    return call(body, [shape((8, 128), F32)], ins, [], name, after)[0]


def shift_term(stats, means, masked):
    lines = filled(split3(stats[0:1, :] - means[0:1, :]), stats.shape[1]).astype(BF16)
    rows = lax.dot_general(
        lines, masked[...], (((1,), (1,)), ((), ())), preferred_element_type=F32
    )
    return rows[0:1] + rows[1:2] + rows[2:3]


def times_masked(columns, at, masked):
    return lax.dot_general(
        columns[at:at + 256, :], masked[...], (((1,), (1,)), ((), ())), preferred_element_type=F32
    )


def grad_kernel(
    first, rows, add, with_base, place, columns, stats, means, own, one, two, three_on, *rest
):
    out, masked = rest[-2:]
    for d, piece in enumerate((own, one, two, three_on)):
        row = pl.multiple_of((place[2] + 4 - d) % 4 * QUARTER, QUARTER)
        masked[pl.ds(row, QUARTER), :] = piece[0:QUARTER, :]
    shift = shift_term(stats, means, masked)
    for at in range(first, first + rows, 256):
        product = times_masked(columns, at, masked) + shift
        if add:
            product = product + rest[0][at:at + 256, :]
        if with_base:
            product = GRAD_SCALE * product + rest[1][at:at + 256, :]
        out[at - first:at - first + 256, :] = product.astype(out.dtype)


def grad_part(place, inputs, pieces, previous, first, rows, dtype, name, after=(), base=None):
    columns, stats, means = inputs
    ins = [place, columns, stats, means] + pieces
    ins += [a for a in (previous, base) if a is not None]
    return call(
        functools.partial(
            grad_kernel, first, rows, previous is not None, base is not None
        ),
        [shape((rows, FEATS), dtype)],
        ins,
        [pltpu.VMEM((FEATS, columns.shape[1]), BF16)],
        name,
        after,
    )[0]


def per_device(student, teacher):
    row_index = lax.axis_index("row")
    col_index = lax.axis_index("col")
    core = col_index % 2
    chip = col_index // 2
    place = jnp.stack([chip, core, chip % 4, chip // 4, row_index // 2]).astype(jnp.int32)

    sibling = swap_cores(student)
    own_a = lax.dynamic_slice_in_dim(student, core * HALF, HALF, 1)
    x_lo_a = shift_row(own_a, 1, 0)
    x_hi_a = shift_row(own_a, -1, 0)
    own_b = lax.dynamic_slice_in_dim(sibling, core * HALF, HALF, 1)
    x_lo_b = shift_row(own_b, 1, 0)
    x_hi_b = shift_row(own_b, -1, 0)
    z_own_a = shift_row(own_a, 0, 1)
    z_own_b = shift_row(own_b, 0, 1)
    rows_t, own_stats, parts = center_own(student, sibling, teacher, [x_lo_a])
    x_lo_a, x_lo_b = lax.optimization_barrier((x_lo_a, x_lo_b))
    x_far_a = shift_row(x_lo_a, 1, 0)
    x_far_b = shift_row(x_hi_b, -1, 0)
    near = [own_a, own_b, x_lo_a, x_lo_b, x_hi_a, x_hi_b, z_own_a, z_own_b]

    near_sums, near_columns, near_stats = partial_sums(
        place, rows_t, own_stats, near, True, "partial_near"
    )
    z_own = join(z_own_a, z_own_b, [near_stats])
    z_lo = shift_row(z_own, 1, 0)
    z_hi = shift_row(z_own, -1, 0)
    x_far = join(x_far_a, x_far_b, [z_own])
    z_far = shift_row(x_far, 0, 1)
    far = [x_far, z_lo, z_hi, z_far]
    near_sums[1], near_sums[3] = shift_y(near_sums[1], 1), shift_y(near_sums[3], 3)
    near_sums = list(lax.optimization_barrier(tuple(near_sums)))
    near_sums[2] = shift_y(near_sums[2], 2)
    far_sums, far_columns, far_stats = partial_sums(
        place, rows_t, own_stats, far, False, "partial_far"
    )
    for d in (1, 3, 2):
        far_sums[d] = shift_y(far_sums[d], d)

    plane, message, local, row_local = combine_y(
        place, parts, near_sums, True, "combine_y_near", [far_sums[0]]
    )
    far_plane, far_message, far_local = combine_y(
        place, parts, far_sums, False, "combine_y_far", [plane]
    )
    near_masked, parts, near_means, row_offsets, row_stats = combine_z(
        place, plane, local, row_local, swap_z_hi(message), parts, True,
        "combine_z_near",
        [far_plane],
    )
    near_pieces = sent_round(near_masked)
    far_masked, parts, far_means = combine_z(
        place, far_plane, far_local, row_offsets, swap_z_hi(far_message), parts, False,
        "combine_z_far", near_pieces[1:],
    )
    far_pieces = sent_round(far_masked)

    base = base_part(student, teacher, row_stats, [far_masked])
    near_inputs = (near_columns, near_stats, near_means)
    far_inputs = (far_columns, far_stats, far_means)
    grads = grad_part(
        place, near_inputs, near_pieces, None, 0, CHIP_IMAGES, F32, "grad_near", [base]
    )
    parts = pair_sum(pair_sum(parts, 2, 0), 4, 0)
    outgoing = grad_part(
        place, far_inputs, far_pieces, grads, IMAGES, IMAGES, BF16, "grad_far_sent", [parts]
    )
    incoming = swap_cores(outgoing)
    kept = grad_part(
        place, far_inputs, far_pieces, grads, 0, IMAGES, F32, "grad_far_kept", [outgoing], base
    )
    parts = four_sum(parts, (1, 0), (0, 1), add_four_kernel, "four_sum")
    total_loss = four_sum(parts, (0, 2), (0, 4), loss_kernel, "loss", [kept])
    return (kept + GRAD_SCALE * incoming.astype(F32), total_loss[0, 0])


def solution(mesh):
    in_specs = (P("col", "row"), P("col", "row"))
    out_specs = (P("col", "row"), P())
    return jax.shard_map(
        per_device, mesh=mesh, in_specs=in_specs, out_specs=out_specs, check_vma=False
    )
```

```python
import functools

import jax
import jax.numpy as jnp
from jax import lax
from jax.experimental import pallas as pl
from jax.experimental.pallas import tpu as pltpu
from jax.sharding import PartitionSpec as P

F32 = jnp.float32
BF16 = jnp.bfloat16
IMAGES, FEATS, CHIPS = 768, 512, 8
BATCH = IMAGES * 16
CHIP_IMAGES = 2 * IMAGES
HALF = FEATS // 2
STAT_ROWS = 16
GRAD_SCALE = BATCH / (16.0 * (BATCH - 1))

QUARTER = FEATS // 4
UPPER = QUARTER // 2
VMEM = pl.BlockSpec(memory_space=pltpu.VMEM)
SMEM = pl.BlockSpec(memory_space=pltpu.SMEM)
ANY = pl.BlockSpec(memory_space=pl.ANY)


def shift_row(block, dx, dz):
    pairs = [(2 * x + z, 2 * ((x + dx) % 4) + (z + dz) % 2) for x in range(4) for z in range(2)]
    return lax.ppermute(block, "row", pairs)


def flip(block, z_lo, core):
    pairs = []
    for row in range(8):
        for col in range(16):
            pairs.append((16 * row + col, 16 * (row ^ z_lo) + (col ^ core)))
    return lax.ppermute(block, ("row", "col"), pairs)


def swap_cores(block):
    return lax.ppermute(block, "col", [(i, i ^ 1) for i in range(16)])


def shift_y(block, dy):
    pairs = [
        (8 * z + 2 * y + core, 8 * z + 2 * ((y + dy) % 4) + core)
        for z in range(2) for y in range(4) for core in range(2)
    ]
    return lax.ppermute(block, "col", pairs)


def sent_round(block):
    two, one, three_on = [shift_y(block, d) for d in (2, 1, 3)]
    return [block, one, two, three_on]


def swap_z_hi(block):
    return lax.ppermute(block, "col", [(i, i ^ 8) for i in range(16)])


def call(body, outs, ins, scratch, name, after=(), flops=0):
    count, waits = len(ins), len(after)

    def kernel(*refs):
        body(*refs[:count], *refs[count + waits:])

    return pl.pallas_call(
        kernel,
        out_shape=tuple(outs),
        in_specs=[SMEM if a.dtype == jnp.int32 else VMEM for a in ins] + [ANY] * waits,
        out_specs=tuple(VMEM for _ in outs),
        scratch_shapes=scratch,
        compiler_params=pltpu.CompilerParams(vmem_limit_bytes=16 * 2**20),
        cost_estimate=pl.CostEstimate(flops=flops, bytes_accessed=0, transcendentals=0),
        name=name,
    )(*ins, *after)


def shape(dims, dtype):
    return jax.ShapeDtypeStruct(dims, dtype)


def layout(chunks):
    places, column, at = [], 0, 0
    while at < len(chunks):
        rows, width = chunks[at].shape
        count = CHIP_IMAGES // rows
        for part in range(count):
            places.append((at + part, part * rows, column))
        column += width
        at += count
    return places, column


def split3(value):
    high = value.astype(BF16).astype(F32)
    middle = (value - high).astype(BF16).astype(F32)
    return [high, middle, value - high - middle]


def column_sum(ref):
    ones = jnp.ones((8, ref.shape[0]), BF16)
    return jnp.dot(ones, ref[...], preferred_element_type=F32)[0:1]


def center_into(target, first, column, ref, mean):
    width = ref.shape[1]
    step = 128

    def body(i, carry):
        at = pl.multiple_of(i * step, step)
        block = ref[pl.ds(at, step), :].astype(F32) - mean
        target[pl.ds(first + at, step), column:column + width] = block.astype(BF16)
        return carry

    lax.fori_loop(0, ref.shape[0] // step, body, 0)


def fill_columns(places, refs, columns, stats):
    means = {}
    for at, _, column in places:
        means[column] = means.get(column, 0.0) + column_sum(refs[at])
    for column, total in means.items():
        mean = total / CHIP_IMAGES
        stats[0:1, column:column + mean.shape[1]] = mean
        means[column] = mean
    for at, first, column in places:
        center_into(columns, first, column, refs[at], means[column])


def center_rows(target, first, ref, mean):
    step = 128

    def body(i, total):
        at = pl.multiple_of(i * step, step)
        block = ref[pl.ds(at, step), :].astype(F32) - mean
        target[pl.ds(first + at, step), :] = block.astype(BF16)
        return total + jnp.sum((block * block).reshape(step // 8, 8, FEATS), axis=0)

    total = lax.fori_loop(0, ref.shape[0] // step, body, jnp.zeros((8, FEATS), F32))
    return jnp.sum(total, axis=0, keepdims=True)


def padded(lines, width):
    pad = width - lines[0].shape[1]
    return [jnp.concatenate([line, jnp.zeros((line.shape[0], pad), F32)], axis=1) for line in lines]


def filled(lines, width):
    count = sum(line.shape[0] for line in lines)
    lines = lines + [jnp.zeros((-count % STAT_ROWS, width), F32)]
    return jnp.concatenate([line for line in lines if line.shape[0]], axis=0)


def rows_kernel(own, sibling, teacher, rows_t, row_stats, parts, rows):
    row_mean = (column_sum(own) + column_sum(sibling)) / CHIP_IMAGES
    squares = center_rows(rows, 0, own, row_mean) + center_rows(rows, IMAGES, sibling, row_mean)
    for at in range(0, FEATS, 128):
        rows_t[at:at + 128, :] = rows[:, at:at + 128].T
    row_stats[...] = jnp.concatenate([row_mean, squares, jnp.zeros((6, FEATS), F32)], axis=0)

    def body(i, total):
        at = pl.ds(pl.multiple_of(i * 128, 128), 128)
        diff = own[at, :].astype(F32) - teacher[at, :].astype(F32)
        return total + jnp.sum((diff * diff).reshape(16, 8, FEATS), axis=0)

    total = lax.fori_loop(0, IMAGES // 128, body, jnp.zeros((8, FEATS), F32))
    lanes = lax.broadcasted_iota(jnp.int32, parts.shape, 1)
    parts[...] = jnp.where(lanes == 1, jnp.sum(total, keepdims=True), 0.0)


def center_own(own, sibling, teacher, after):
    return call(
        rows_kernel,
        [shape((FEATS, CHIP_IMAGES), BF16), shape((8, FEATS), F32), shape((8, 128), F32)],
        [own, sibling, teacher],
        [pltpu.VMEM((CHIP_IMAGES, FEATS), BF16)],
        "center_own",
        after,
    )


def join_kernel(first, second, out):
    out[0:IMAGES, :] = first[...]
    out[IMAGES:CHIP_IMAGES, :] = second[...]


def join(first, second, after=()):
    return call(
        join_kernel, [shape((CHIP_IMAGES, HALF), BF16)], [first, second], [], "join", after
    )[0]


def base_kernel(student, teacher, row_stats, out):
    mean, spread = row_stats[0:1, :], row_stats[1:2, :]
    scale = jnp.where(spread < 1.0, 25.0 * BATCH / 64.0 / (spread * (BATCH - 1)), 0.0)

    def body(i, carry):
        at = pl.ds(pl.multiple_of(i * 64, 64), 64)
        value = student[at, :].astype(F32)
        diff = value - teacher[at, :].astype(F32)
        out[at, :] = (25.0 / 32.0) * diff - scale * (value - mean)
        return carry

    lax.fori_loop(0, IMAGES // 64, body, 0)


def base_part(student, teacher, row_stats, after):
    ins = [student, teacher, row_stats]
    return call(base_kernel, [shape((IMAGES, FEATS), F32)], ins, [], "base", after)[0]


def partial_kernel(places, width, count, with_rows, *refs):
    place, rows_t, row_stats = refs[:3]
    chunks = refs[3:3 + count]
    pieces = refs[3 + count:7 + count]
    columns, stats, sums = refs[7 + count:]
    fill_columns(places, chunks, columns, stats)
    for at in range(0, width, 256):
        sums[:, at:at + 256] = jnp.dot(
            rows_t[...], columns[:, at:at + 256], preferred_element_type=F32
        )
    lines = split3(stats[0:1, :])
    if with_rows:
        lines += padded(split3(row_stats[0:1, :]) + split3(row_stats[1:2, :]), width)
    block = filled(lines, width)
    for d in range(4):
        first = pl.multiple_of((place[2] + d) % 4 * QUARTER, QUARTER)
        pieces[d][0:QUARTER, :] = sums[pl.ds(first, QUARTER), :].astype(pieces[d].dtype)
        pieces[d][QUARTER:QUARTER + STAT_ROWS, :] = block.astype(pieces[d].dtype)


def partial_sums(place, rows_t, row_stats, chunks, with_rows, name, after=()):
    places, width = layout(chunks)
    rows = QUARTER + STAT_ROWS
    *pieces, columns, stats = call(
        functools.partial(partial_kernel, places, width, len(chunks), with_rows),
        [shape((rows, width), F32)]
        + [shape((rows, width), BF16)] * 3
        + [shape((CHIP_IMAGES, width), BF16), shape((8, width), F32)],
        [place, rows_t, row_stats] + chunks,
        [pltpu.VMEM((FEATS, width), F32)],
        name,
        after,
        flops=40 * CHIP_IMAGES * FEATS * width,
    )
    return pieces, columns, stats


def spread_out(local):
    mean = jnp.sum(local, axis=0, keepdims=True) / CHIPS
    return local - mean, mean


def mean_term(row_offsets, col_offsets):
    return CHIP_IMAGES * lax.dot_general(
        row_offsets,
        col_offsets,
        (((0,), (0,)), ((), ())),
        precision=lax.Precision.HIGHEST,
        preferred_element_type=F32,
    )


def three(stats, first):
    return stats[first:first + 1] + stats[first + 1:first + 2] + stats[first + 2:first + 3]


def combine_y_kernel(
    with_rows, place, parts, own, one, two, three_on, plane, upper, message, local, *row_local
):
    width = own.shape[1]
    columns = jnp.zeros((4, width), F32)
    rows = jnp.zeros((4, FEATS), F32)
    squares = jnp.zeros((1, FEATS), F32)
    total = own[0:QUARTER, :]
    for d, piece in enumerate((own, one, two, three_on)):
        if d:
            total = total + piece[0:QUARTER, :].astype(F32)
        at = (place[2] + 4 - d) % 4
        stats = piece[QUARTER:QUARTER + STAT_ROWS, :].astype(F32)
        here = lax.broadcasted_iota(jnp.int32, columns.shape, 0) == at
        columns = jnp.where(here, three(stats, 0), columns)
        if with_rows:
            here = lax.broadcasted_iota(jnp.int32, rows.shape, 0) == at
            rows = jnp.where(here, three(stats[:, 0:FEATS], 3), rows)
            squares = squares + three(stats[:, 0:FEATS], 6)

    def rounded(value):
        high, middle, low = split3(value)
        low = low.astype(BF16).astype(F32)
        return [high, middle, low], high + middle + low

    plane[...] = total.astype(BF16)
    upper[...] = total[0:UPPER].astype(BF16)
    message[0:QUARTER - UPPER, :] = total[UPPER:].astype(BF16)
    lines, local[0:4, :] = rounded(columns)
    if with_rows:
        row_lines, row_local[0][0:4, :] = rounded(rows)
        square_lines, row_local[0][4:5, :] = rounded(squares)
        part_lines, _ = rounded(parts[0:1, :])
        lines = lines + padded(row_lines + square_lines, width) + padded(part_lines, width)
    block = filled(lines, width)
    message[QUARTER - UPPER:, :] = block.astype(BF16)


def combine_y(place, parts, pieces, with_rows, name, after=()):
    width = pieces[0].shape[1]
    rows = QUARTER - UPPER + (2 if with_rows else 1) * STAT_ROWS
    outs = [shape((QUARTER, width), BF16), shape((UPPER, width), BF16)]
    outs += [shape((rows, width), BF16), shape((8, width), F32)]
    outs += [shape((8, FEATS), F32)] if with_rows else []
    return call(
        functools.partial(combine_y_kernel, with_rows), outs, [place, parts] + pieces, [], name, after
    )


def all_chips(place, mine, theirs):
    low = place[3] == 0
    return jnp.concatenate([jnp.where(low, mine, theirs), jnp.where(low, theirs, mine)], axis=0)


def combine_z_kernel(
    with_rows, place, plane, local, rows, upper, received, parts, masked, part, means, *more
):
    stats = received[QUARTER - UPPER:, :].astype(F32)
    theirs = stats[0:4] + stats[4:8] + stats[8:12]
    col_off, col_mean = spread_out(all_chips(place, local[0:4, :], theirs))
    means[...] = jnp.broadcast_to(col_mean, means.shape)
    row_offsets = rows
    if with_rows:
        row_offsets, row_stats = more
        other_parts = three(stats[:, 0:128], 27)
        stats = stats[:, 0:FEATS]
        theirs = stats[12:16] + stats[16:20] + stats[20:24]
        row_off, row_mean = spread_out(all_chips(place, rows[0:4, :], theirs))
        squares = rows[4:5, :] + three(stats, 24)
        squares = squares + CHIP_IMAGES * jnp.sum(row_off * row_off, axis=0, keepdims=True)
        variance = squares / (BATCH - 1)
        row_offsets[...] = row_off
        spread = jnp.sqrt(variance + 0.0001)
        row_stats[...] = jnp.concatenate([row_mean, spread, jnp.zeros((6, FEATS), F32)], axis=0)
    block = pl.multiple_of(place[2] * QUARTER, QUARTER)
    term = mean_term(row_offsets[:, pl.ds(block, QUARTER)], col_off)
    other = [upper[...].astype(F32), received[0:QUARTER - UPPER, :].astype(F32)]
    covar = plane[...].astype(F32) + jnp.concatenate(other, axis=0)
    covar = (covar + term) / (BATCH - 1)
    if with_rows:
        row_ids = place[2] * QUARTER + lax.broadcasted_iota(jnp.int32, covar.shape, 0)
        col_ids = lax.broadcasted_iota(jnp.int32, covar.shape, 1)
        on_diagonal = (col_ids < HALF) & (row_ids == col_ids + place[1] * HALF)
        covar = jnp.where(on_diagonal, F32(0.0), covar)
    lanes = lax.broadcasted_iota(jnp.int32, part.shape, 1)
    found = jnp.where(lanes == 0, jnp.sum(covar * covar, keepdims=True), 0.0)
    if with_rows:
        var_part = jnp.sum(jnp.maximum(0.0, 1.0 - spread), keepdims=True) / 8
        found = found + jnp.where(lanes == 2, var_part, 0.0) + other_parts
    part[...] = parts[...] + found
    masked[0:QUARTER, :] = covar.astype(BF16)


def combine_z(place, plane, local, rows, upper, received, parts, with_rows, name, after=()):
    width = plane.shape[1]
    outs = [shape((QUARTER, width), BF16), shape((8, 128), F32), shape((8, width), F32)]
    outs += [shape((8, FEATS), F32)] * 2 if with_rows else []
    ins = [place, plane, local, rows, upper, received, parts]
    return call(functools.partial(combine_z_kernel, with_rows), outs, ins, [], name, after)


def add_kernel(one, two, out):
    out[...] = one[...] + two[...]


def add_four_kernel(one, two, three_on, four, out):
    out[...] = (one[...] + two[...]) + (three_on[...] + four[...])


def loss_kernel(one, two, three_on, four, out):
    total = (one[...] + two[...]) + (three_on[...] + four[...])
    loss = total[0:1, 0:1] + 25.0 * (total[0:1, 1:2] / BATCH + total[0:1, 2:3])
    out[...] = loss / (8 * FEATS)


def flip(parts, row_bits, col_bits):
    if not row_bits:
        return lax.ppermute(parts, "col", [(i, i ^ col_bits) for i in range(16)])
    if not col_bits:
        return lax.ppermute(parts, "row", [(i, i ^ row_bits) for i in range(8)])
    pairs = [
        (16 * row + col, 16 * (row ^ row_bits) + (col ^ col_bits))
        for row in range(8) for col in range(16)
    ]
    return lax.ppermute(parts, ("row", "col"), pairs)


def pair_sum(parts, row_bits, col_bits, after=()):
    ins = [parts, flip(parts, row_bits, col_bits)]
    return call(add_kernel, [shape((8, 128), F32)], ins, [], "pair_sum", after)[0]


def four_sum(parts, first, second, body, name, out=(8, 128), after=()):
    both = (first[0] | second[0], first[1] | second[1])
    ins = [parts] + [flip(parts, *bits) for bits in (first, second, both)]
    return call(body, [shape(out, F32)], ins, [], name, after)[0]


def shift_term(stats, means, masked):
    lines = filled(split3(stats[0:1, :] - means[0:1, :]), stats.shape[1]).astype(BF16)
    rows = lax.dot_general(
        lines, masked[...], (((1,), (1,)), ((), ())), preferred_element_type=F32
    )
    return rows[0:1] + rows[1:2] + rows[2:3]


def times_masked(columns, at, masked):
    return lax.dot_general(
        columns[at:at + 256, :], masked[...], (((1,), (1,)), ((), ())), preferred_element_type=F32
    )


def grad_kernel(
    first, rows, add, with_base, place, columns, stats, means, own, one, two, three_on, *rest
):
    out, masked = rest[-2:]
    for d, piece in enumerate((own, one, two, three_on)):
        row = pl.multiple_of((place[2] + 4 - d) % 4 * QUARTER, QUARTER)
        masked[pl.ds(row, QUARTER), :] = piece[0:QUARTER, :]
    shift = shift_term(stats, means, masked)
    for at in range(first, first + rows, 256):
        product = times_masked(columns, at, masked) + shift
        if add:
            product = product + rest[0][at:at + 256, :]
        if with_base:
            product = GRAD_SCALE * product + rest[1][at:at + 256, :]
        out[at - first:at - first + 256, :] = product.astype(out.dtype)


def grad_part(place, inputs, pieces, previous, first, rows, dtype, name, after=(), base=None):
    columns, stats, means = inputs
    ins = [place, columns, stats, means] + pieces
    ins += [a for a in (previous, base) if a is not None]
    return call(
        functools.partial(
            grad_kernel, first, rows, previous is not None, base is not None
        ),
        [shape((rows, FEATS), dtype)],
        ins,
        [pltpu.VMEM((FEATS, columns.shape[1]), BF16)],
        name,
        after,
    )[0]


def per_device(student, teacher):
    row_index = lax.axis_index("row")
    col_index = lax.axis_index("col")
    core = col_index % 2
    chip = col_index // 2
    place = jnp.stack([chip, core, chip % 4, chip // 4, row_index // 2]).astype(jnp.int32)

    sibling = swap_cores(student)
    own_a = lax.dynamic_slice_in_dim(student, core * HALF, HALF, 1)
    x_lo_a = shift_row(own_a, 1, 0)
    x_hi_a = shift_row(own_a, -1, 0)
    own_b = lax.dynamic_slice_in_dim(sibling, core * HALF, HALF, 1)
    x_lo_b = shift_row(own_b, 1, 0)
    x_hi_b = shift_row(own_b, -1, 0)
    z_own_a = shift_row(own_a, 0, 1)
    z_own_b = shift_row(own_b, 0, 1)
    rows_t, own_stats, parts = center_own(student, sibling, teacher, [x_lo_a])
    x_lo_a, x_lo_b = lax.optimization_barrier((x_lo_a, x_lo_b))
    x_far_a = shift_row(x_lo_a, 1, 0)
    x_far_b = shift_row(x_hi_b, -1, 0)
    near = [own_a, own_b, x_lo_a, x_lo_b, x_hi_a, x_hi_b, z_own_a, z_own_b]

    near_sums, near_columns, near_stats = partial_sums(
        place, rows_t, own_stats, near, True, "partial_near"
    )
    z_own = join(z_own_a, z_own_b, [near_stats])
    z_lo = shift_row(z_own, 1, 0)
    z_hi = shift_row(z_own, -1, 0)
    x_far = join(x_far_a, x_far_b, [z_own])
    z_far = shift_row(x_far, 0, 1)
    far = [x_far, z_lo, z_hi, z_far]
    near_sums[1], near_sums[3] = shift_y(near_sums[1], 1), shift_y(near_sums[3], 3)
    near_sums = list(lax.optimization_barrier(tuple(near_sums)))
    near_sums[2] = shift_y(near_sums[2], 2)
    far_sums, far_columns, far_stats = partial_sums(
        place, rows_t, own_stats, far, False, "partial_far"
    )
    plane, upper, message, local, row_local = combine_y(
        place, parts, near_sums, True, "combine_y_near", [far_sums[0]]
    )
    *far_sums, plane = lax.optimization_barrier((*far_sums, plane))
    for d in (1, 3, 2):
        far_sums[d] = shift_y(far_sums[d], d)
    near_masked, parts, near_means, row_offsets, row_stats = combine_z(
        place, plane, local, row_local, swap_z_hi(upper), swap_z_hi(message), parts, True,
        "combine_z_near", [far_sums[1]],
    )
    near_pieces = sent_round(near_masked)
    far_plane, far_upper, far_message, far_local = combine_y(
        place, parts, far_sums, False, "combine_y_far", [near_masked]
    )
    far_masked, parts, far_means = combine_z(
        place, far_plane, far_local, row_offsets, swap_z_hi(far_upper), swap_z_hi(far_message),
        parts, False,
        "combine_z_far", near_pieces[1:],
    )
    far_pieces = sent_round(far_masked)

    base = base_part(student, teacher, row_stats, [far_masked])
    near_inputs = (near_columns, near_stats, near_means)
    far_inputs = (far_columns, far_stats, far_means)
    grads = grad_part(
        place, near_inputs, near_pieces, None, 0, CHIP_IMAGES, F32, "grad_near", [base]
    )
    parts = pair_sum(pair_sum(parts, 2, 0), 4, 0)
    outgoing = grad_part(
        place, far_inputs, far_pieces, grads, IMAGES, IMAGES, BF16, "grad_far_sent", [parts]
    )
    incoming = swap_cores(outgoing)
    kept = grad_part(
        place, far_inputs, far_pieces, grads, 0, IMAGES, F32, "grad_far_kept", [outgoing], base
    )
    parts = four_sum(parts, (1, 0), (0, 1), add_four_kernel, "four_sum")
    total_loss = four_sum(parts, (0, 2), (0, 4), loss_kernel, "loss", (1, 1), [kept])
    return (kept + GRAD_SCALE * incoming.astype(F32), total_loss[0, 0])


def solution(mesh):
    in_specs = (P("col", "row"), P("col", "row"))
    out_specs = (P("col", "row"), P())
    return jax.shard_map(
        per_device, mesh=mesh, in_specs=in_specs, out_specs=out_specs, check_vma=False
    )
```

```python
import functools

import jax
import jax.numpy as jnp
from jax import lax
from jax.experimental import pallas as pl
from jax.experimental.pallas import tpu as pltpu
from jax.sharding import PartitionSpec as P

F32 = jnp.float32
BF16 = jnp.bfloat16
IMAGES, FEATS, CHIPS = 768, 512, 8
BATCH = IMAGES * 16
CHIP_IMAGES = 2 * IMAGES
HALF = FEATS // 2
STAT_ROWS = 16
GRAD_SCALE = BATCH / (16.0 * (BATCH - 1))

QUARTER = FEATS // 4
UPPER = QUARTER // 2
VMEM = pl.BlockSpec(memory_space=pltpu.VMEM)
SMEM = pl.BlockSpec(memory_space=pltpu.SMEM)
ANY = pl.BlockSpec(memory_space=pl.ANY)


def shift_row(block, dx, dz):
    pairs = [(2 * x + z, 2 * ((x + dx) % 4) + (z + dz) % 2) for x in range(4) for z in range(2)]
    return lax.ppermute(block, "row", pairs)


def flip(block, z_lo, core):
    pairs = []
    for row in range(8):
        for col in range(16):
            pairs.append((16 * row + col, 16 * (row ^ z_lo) + (col ^ core)))
    return lax.ppermute(block, ("row", "col"), pairs)


def swap_cores(block):
    return lax.ppermute(block, "col", [(i, i ^ 1) for i in range(16)])


def shift_y(block, dy):
    pairs = [
        (8 * z + 2 * y + core, 8 * z + 2 * ((y + dy) % 4) + core)
        for z in range(2) for y in range(4) for core in range(2)
    ]
    return lax.ppermute(block, "col", pairs)


def sent_round(block):
    two, one, three_on = [shift_y(block, d) for d in (2, 1, 3)]
    return [block, one, two, three_on]


def swap_z_hi(block):
    return lax.ppermute(block, "col", [(i, i ^ 8) for i in range(16)])


def call(body, outs, ins, scratch, name, after=(), flops=0):
    count, waits = len(ins), len(after)

    def kernel(*refs):
        body(*refs[:count], *refs[count + waits:])

    return pl.pallas_call(
        kernel,
        out_shape=tuple(outs),
        in_specs=[SMEM if a.dtype == jnp.int32 else VMEM for a in ins] + [ANY] * waits,
        out_specs=tuple(VMEM for _ in outs),
        scratch_shapes=scratch,
        compiler_params=pltpu.CompilerParams(vmem_limit_bytes=16 * 2**20),
        cost_estimate=pl.CostEstimate(flops=flops, bytes_accessed=0, transcendentals=0),
        name=name,
    )(*ins, *after)


def shape(dims, dtype):
    return jax.ShapeDtypeStruct(dims, dtype)


def layout(chunks):
    places, column, at = [], 0, 0
    while at < len(chunks):
        rows, width = chunks[at].shape
        count = CHIP_IMAGES // rows
        for part in range(count):
            places.append((at + part, part * rows, column))
        column += width
        at += count
    return places, column


def split3(value):
    high = value.astype(BF16).astype(F32)
    middle = (value - high).astype(BF16).astype(F32)
    return [high, middle, value - high - middle]


def column_sum(ref):
    ones = jnp.ones((8, ref.shape[0]), BF16)
    return jnp.dot(ones, ref[...], preferred_element_type=F32)[0:1]


def center_into(target, first, column, ref, mean):
    width = ref.shape[1]
    step = 128

    def body(i, carry):
        at = pl.multiple_of(i * step, step)
        block = ref[pl.ds(at, step), :].astype(F32) - mean
        target[pl.ds(first + at, step), column:column + width] = block.astype(BF16)
        return carry

    lax.fori_loop(0, ref.shape[0] // step, body, 0)


def fill_columns(places, refs, columns, stats):
    means = {}
    for at, _, column in places:
        means[column] = means.get(column, 0.0) + column_sum(refs[at])
    for column, total in means.items():
        mean = total / CHIP_IMAGES
        stats[0:1, column:column + mean.shape[1]] = mean
        means[column] = mean
    for at, first, column in places:
        center_into(columns, first, column, refs[at], means[column])


def center_rows(target, first, ref, mean):
    step = 128

    def body(i, total):
        at = pl.multiple_of(i * step, step)
        block = ref[pl.ds(at, step), :].astype(F32) - mean
        target[pl.ds(first + at, step), :] = block.astype(BF16)
        return total + jnp.sum((block * block).reshape(step // 8, 8, FEATS), axis=0)

    total = lax.fori_loop(0, ref.shape[0] // step, body, jnp.zeros((8, FEATS), F32))
    return jnp.sum(total, axis=0, keepdims=True)


def padded(lines, width):
    pad = width - lines[0].shape[1]
    return [jnp.concatenate([line, jnp.zeros((line.shape[0], pad), F32)], axis=1) for line in lines]


def filled(lines, width):
    count = sum(line.shape[0] for line in lines)
    lines = lines + [jnp.zeros((-count % STAT_ROWS, width), F32)]
    return jnp.concatenate([line for line in lines if line.shape[0]], axis=0)


def rows_kernel(own, sibling, teacher, rows_t, row_stats, parts, rows):
    row_mean = (column_sum(own) + column_sum(sibling)) / CHIP_IMAGES
    squares = center_rows(rows, 0, own, row_mean) + center_rows(rows, IMAGES, sibling, row_mean)
    for at in range(0, FEATS, 128):
        rows_t[at:at + 128, :] = rows[:, at:at + 128].T
    row_stats[...] = jnp.concatenate([row_mean, squares, jnp.zeros((6, FEATS), F32)], axis=0)

    def body(i, total):
        at = pl.ds(pl.multiple_of(i * 128, 128), 128)
        diff = own[at, :].astype(F32) - teacher[at, :].astype(F32)
        return total + jnp.sum((diff * diff).reshape(16, 8, FEATS), axis=0)

    total = lax.fori_loop(0, IMAGES // 128, body, jnp.zeros((8, FEATS), F32))
    lanes = lax.broadcasted_iota(jnp.int32, parts.shape, 1)
    parts[...] = jnp.where(lanes == 1, jnp.sum(total, keepdims=True), 0.0)


def center_own(own, sibling, teacher, after):
    return call(
        rows_kernel,
        [shape((FEATS, CHIP_IMAGES), BF16), shape((8, FEATS), F32), shape((8, 128), F32)],
        [own, sibling, teacher],
        [pltpu.VMEM((CHIP_IMAGES, FEATS), BF16)],
        "center_own",
        after,
    )


def join_kernel(first, second, out):
    out[0:IMAGES, :] = first[...]
    out[IMAGES:CHIP_IMAGES, :] = second[...]


def join(first, second, after=()):
    return call(
        join_kernel, [shape((CHIP_IMAGES, HALF), BF16)], [first, second], [], "join", after
    )[0]


def base_kernel(student, teacher, row_stats, out):
    mean, spread = row_stats[0:1, :], row_stats[1:2, :]
    scale = jnp.where(spread < 1.0, 25.0 * BATCH / 64.0 / (spread * (BATCH - 1)), 0.0)

    def body(i, carry):
        at = pl.ds(pl.multiple_of(i * 64, 64), 64)
        value = student[at, :].astype(F32)
        diff = value - teacher[at, :].astype(F32)
        out[at, :] = (25.0 / 32.0) * diff - scale * (value - mean)
        return carry

    lax.fori_loop(0, IMAGES // 64, body, 0)


def base_part(student, teacher, row_stats, after):
    ins = [student, teacher, row_stats]
    return call(base_kernel, [shape((IMAGES, FEATS), F32)], ins, [], "base", after)[0]


def partial_kernel(places, width, count, with_rows, *refs):
    place, rows_t, row_stats = refs[:3]
    chunks = refs[3:3 + count]
    pieces = refs[3 + count:7 + count]
    columns, stats, sums = refs[7 + count:]
    fill_columns(places, chunks, columns, stats)
    for at in range(0, width, 256):
        sums[:, at:at + 256] = jnp.dot(
            rows_t[...], columns[:, at:at + 256], preferred_element_type=F32
        )
    lines = split3(stats[0:1, :])
    if with_rows:
        lines += padded(split3(row_stats[0:1, :]) + split3(row_stats[1:2, :]), width)
    block = filled(lines, width)
    for d in range(4):
        first = pl.multiple_of((place[2] + d) % 4 * QUARTER, QUARTER)
        pieces[d][0:QUARTER, :] = sums[pl.ds(first, QUARTER), :].astype(pieces[d].dtype)
        pieces[d][QUARTER:QUARTER + STAT_ROWS, :] = block.astype(pieces[d].dtype)


def partial_sums(place, rows_t, row_stats, chunks, with_rows, name, after=()):
    places, width = layout(chunks)
    rows = QUARTER + STAT_ROWS
    *pieces, columns, stats = call(
        functools.partial(partial_kernel, places, width, len(chunks), with_rows),
        [shape((rows, width), F32)]
        + [shape((rows, width), BF16)] * 3
        + [shape((CHIP_IMAGES, width), BF16), shape((8, width), F32)],
        [place, rows_t, row_stats] + chunks,
        [pltpu.VMEM((FEATS, width), F32)],
        name,
        after,
        flops=40 * CHIP_IMAGES * FEATS * width,
    )
    return pieces, columns, stats


def spread_out(local):
    mean = jnp.sum(local, axis=0, keepdims=True) / CHIPS
    return local - mean, mean


def mean_term(row_offsets, col_offsets):
    return CHIP_IMAGES * lax.dot_general(
        row_offsets,
        col_offsets,
        (((0,), (0,)), ((), ())),
        precision=lax.Precision.HIGHEST,
        preferred_element_type=F32,
    )


def three(stats, first):
    return stats[first:first + 1] + stats[first + 1:first + 2] + stats[first + 2:first + 3]


def combine_y_kernel(
    with_rows, place, parts, own, one, two, three_on, plane, upper, message, local, *row_local
):
    width = own.shape[1]
    columns = jnp.zeros((4, width), F32)
    rows = jnp.zeros((4, FEATS), F32)
    squares = jnp.zeros((1, FEATS), F32)
    total = own[0:QUARTER, :]
    for d, piece in enumerate((own, one, two, three_on)):
        if d:
            total = total + piece[0:QUARTER, :].astype(F32)
        at = (place[2] + 4 - d) % 4
        stats = piece[QUARTER:QUARTER + STAT_ROWS, :].astype(F32)
        here = lax.broadcasted_iota(jnp.int32, columns.shape, 0) == at
        columns = jnp.where(here, three(stats, 0), columns)
        if with_rows:
            here = lax.broadcasted_iota(jnp.int32, rows.shape, 0) == at
            rows = jnp.where(here, three(stats[:, 0:FEATS], 3), rows)
            squares = squares + three(stats[:, 0:FEATS], 6)

    def rounded(value):
        high, middle, low = split3(value)
        low = low.astype(BF16).astype(F32)
        return [high, middle, low], high + middle + low

    plane[...] = total.astype(BF16)
    upper[...] = total[0:UPPER].astype(BF16)
    message[0:QUARTER - UPPER, :] = total[UPPER:].astype(BF16)
    lines, local[0:4, :] = rounded(columns)
    if with_rows:
        row_lines, row_local[0][0:4, :] = rounded(rows)
        square_lines, row_local[0][4:5, :] = rounded(squares)
        part_lines, _ = rounded(parts[0:1, :])
        lines = lines + padded(row_lines + square_lines, width) + padded(part_lines, width)
    block = filled(lines, width)
    message[QUARTER - UPPER:, :] = block.astype(BF16)


def combine_y(place, parts, pieces, with_rows, name, after=()):
    width = pieces[0].shape[1]
    rows = QUARTER - UPPER + (2 if with_rows else 1) * STAT_ROWS
    outs = [shape((QUARTER, width), BF16), shape((UPPER, width), BF16)]
    outs += [shape((rows, width), BF16), shape((8, width), F32)]
    outs += [shape((8, FEATS), F32)] if with_rows else []
    return call(
        functools.partial(combine_y_kernel, with_rows), outs, [place, parts] + pieces, [], name, after
    )


def all_chips(place, mine, theirs):
    low = place[3] == 0
    return jnp.concatenate([jnp.where(low, mine, theirs), jnp.where(low, theirs, mine)], axis=0)


def combine_z_kernel(
    with_rows, place, plane, local, rows, upper, received, parts, masked, part, means, *more
):
    stats = received[QUARTER - UPPER:, :].astype(F32)
    theirs = stats[0:4] + stats[4:8] + stats[8:12]
    col_off, col_mean = spread_out(all_chips(place, local[0:4, :], theirs))
    means[...] = jnp.broadcast_to(col_mean, means.shape)
    row_offsets = rows
    if with_rows:
        row_offsets, row_stats = more
        other_parts = three(stats[:, 0:128], 27)
        stats = stats[:, 0:FEATS]
        theirs = stats[12:16] + stats[16:20] + stats[20:24]
        row_off, row_mean = spread_out(all_chips(place, rows[0:4, :], theirs))
        squares = rows[4:5, :] + three(stats, 24)
        squares = squares + CHIP_IMAGES * jnp.sum(row_off * row_off, axis=0, keepdims=True)
        variance = squares / (BATCH - 1)
        row_offsets[...] = row_off
        spread = jnp.sqrt(variance + 0.0001)
        row_stats[...] = jnp.concatenate([row_mean, spread, jnp.zeros((6, FEATS), F32)], axis=0)
    block = pl.multiple_of(place[2] * QUARTER, QUARTER)
    term = mean_term(row_offsets[:, pl.ds(block, QUARTER)], col_off)
    other = [upper[...].astype(F32), received[0:QUARTER - UPPER, :].astype(F32)]
    covar = plane[...].astype(F32) + jnp.concatenate(other, axis=0)
    covar = (covar + term) / (BATCH - 1)
    if with_rows:
        row_ids = place[2] * QUARTER + lax.broadcasted_iota(jnp.int32, covar.shape, 0)
        col_ids = lax.broadcasted_iota(jnp.int32, covar.shape, 1)
        on_diagonal = (col_ids < HALF) & (row_ids == col_ids + place[1] * HALF)
        covar = jnp.where(on_diagonal, F32(0.0), covar)
    lanes = lax.broadcasted_iota(jnp.int32, part.shape, 1)
    found = jnp.where(lanes == 0, jnp.sum(covar * covar, keepdims=True), 0.0)
    if with_rows:
        var_part = jnp.sum(jnp.maximum(0.0, 1.0 - spread), keepdims=True) / 8
        found = found + jnp.where(lanes == 2, var_part, 0.0) + other_parts
    part[...] = parts[...] + found
    masked[0:QUARTER, :] = covar.astype(BF16)


def combine_z(place, plane, local, rows, upper, received, parts, with_rows, name, after=()):
    width = plane.shape[1]
    outs = [shape((QUARTER, width), BF16), shape((8, 128), F32), shape((8, width), F32)]
    outs += [shape((8, FEATS), F32)] * 2 if with_rows else []
    ins = [place, plane, local, rows, upper, received, parts]
    return call(functools.partial(combine_z_kernel, with_rows), outs, ins, [], name, after)


def add_kernel(one, two, out):
    out[...] = one[...] + two[...]


def add_four_kernel(one, two, three_on, four, out):
    out[...] = (one[...] + two[...]) + (three_on[...] + four[...])


def loss_kernel(one, two, three_on, four, out):
    total = (one[...] + two[...]) + (three_on[...] + four[...])
    loss = total[0:1, 0:1] + 25.0 * (total[0:1, 1:2] / BATCH + total[0:1, 2:3])
    out[...] = loss / (8 * FEATS)


def flip(parts, row_bits, col_bits):
    if not row_bits:
        return lax.ppermute(parts, "col", [(i, i ^ col_bits) for i in range(16)])
    if not col_bits:
        return lax.ppermute(parts, "row", [(i, i ^ row_bits) for i in range(8)])
    pairs = [
        (16 * row + col, 16 * (row ^ row_bits) + (col ^ col_bits))
        for row in range(8) for col in range(16)
    ]
    return lax.ppermute(parts, ("row", "col"), pairs)


def pair_sum(parts, row_bits, col_bits, after=()):
    ins = [parts, flip(parts, row_bits, col_bits)]
    return call(add_kernel, [shape((8, 128), F32)], ins, [], "pair_sum", after)[0]


def four_sum(parts, first, second, body, name, out=(8, 128), after=()):
    both = (first[0] | second[0], first[1] | second[1])
    ins = [parts] + [flip(parts, *bits) for bits in (first, second, both)]
    return call(body, [shape(out, F32)], ins, [], name, after)[0]


def shift_term(stats, means, masked):
    lines = filled(split3(stats[0:1, :] - means[0:1, :]), stats.shape[1]).astype(BF16)
    rows = lax.dot_general(
        lines, masked[...], (((1,), (1,)), ((), ())), preferred_element_type=F32
    )
    return rows[0:1] + rows[1:2] + rows[2:3]


def times_masked(columns, at, masked):
    return lax.dot_general(
        columns[at:at + 256, :], masked[...], (((1,), (1,)), ((), ())), preferred_element_type=F32
    )


def grad_kernel(
    first, rows, add, with_base, place, columns, stats, means, own, one, two, three_on, *rest
):
    out, masked = rest[-2:]
    for d, piece in enumerate((own, one, two, three_on)):
        row = pl.multiple_of((place[2] + 4 - d) % 4 * QUARTER, QUARTER)
        masked[pl.ds(row, QUARTER), :] = piece[0:QUARTER, :]
    shift = shift_term(stats, means, masked)
    for at in range(first, first + rows, 256):
        product = times_masked(columns, at, masked) + shift
        if add:
            product = product + rest[0][at:at + 256, :]
        if with_base:
            product = GRAD_SCALE * product + rest[1][at:at + 256, :]
        out[at - first:at - first + 256, :] = product.astype(out.dtype)


def grad_part(place, inputs, pieces, previous, first, rows, dtype, name, after=(), base=None):
    columns, stats, means = inputs
    ins = [place, columns, stats, means] + pieces
    ins += [a for a in (previous, base) if a is not None]
    return call(
        functools.partial(
            grad_kernel, first, rows, previous is not None, base is not None
        ),
        [shape((rows, FEATS), dtype)],
        ins,
        [pltpu.VMEM((FEATS, columns.shape[1]), BF16)],
        name,
        after,
    )[0]


def per_device(student, teacher):
    row_index = lax.axis_index("row")
    col_index = lax.axis_index("col")
    core = col_index % 2
    chip = col_index // 2
    place = jnp.stack([chip, core, chip % 4, chip // 4, row_index // 2]).astype(jnp.int32)

    sibling = swap_cores(student)
    own_a = lax.dynamic_slice_in_dim(student, core * HALF, HALF, 1)
    x_lo_a = shift_row(own_a, 1, 0)
    x_hi_a = shift_row(own_a, -1, 0)
    own_b = lax.dynamic_slice_in_dim(sibling, core * HALF, HALF, 1)
    x_lo_b = shift_row(own_b, 1, 0)
    x_hi_b = shift_row(own_b, -1, 0)
    z_own_a = shift_row(own_a, 0, 1)
    z_own_b = shift_row(own_b, 0, 1)
    rows_t, own_stats, parts = center_own(student, sibling, teacher, [x_lo_a])
    x_next, own_stats = lax.optimization_barrier((x_lo_a, own_stats))
    x_far_a = shift_row(x_next, 1, 0)
    x_far_b = shift_row(x_hi_b, -1, 0)
    near = [own_a, own_b, x_lo_a, x_lo_b, x_hi_a, x_hi_b, z_own_a, z_own_b]

    near_sums, near_columns, near_stats = partial_sums(
        place, rows_t, own_stats, near, True, "partial_near"
    )
    z_own = join(z_own_a, z_own_b, [near_stats])
    z_lo = shift_row(z_own, 1, 0)
    z_hi = shift_row(z_own, -1, 0)
    x_far = join(x_far_a, x_far_b, [z_own])
    z_far = shift_row(x_far, 0, 1)
    far = [x_far, z_lo, z_hi, z_far]
    near_sums[1], near_sums[3] = shift_y(near_sums[1], 1), shift_y(near_sums[3], 3)
    near_sums = list(lax.optimization_barrier(tuple(near_sums)))
    near_sums[2] = shift_y(near_sums[2], 2)
    far_sums, far_columns, far_stats = partial_sums(
        place, rows_t, own_stats, far, False, "partial_far"
    )
    plane, upper, message, local, row_local = combine_y(
        place, parts, near_sums, True, "combine_y_near", [far_sums[0]]
    )
    for d in (1, 3, 2):
        far_sums[d] = shift_y(far_sums[d], d)
    near_masked, parts, near_means, row_offsets, row_stats = combine_z(
        place, plane, local, row_local, swap_z_hi(upper), swap_z_hi(message), parts, True,
        "combine_z_near", [far_sums[1]],
    )
    near_pieces = sent_round(near_masked)
    far_plane, far_upper, far_message, far_local = combine_y(
        place, parts, far_sums, False, "combine_y_far", [near_masked]
    )
    far_masked, parts, far_means = combine_z(
        place, far_plane, far_local, row_offsets, swap_z_hi(far_upper), swap_z_hi(far_message),
        parts, False,
        "combine_z_far", near_pieces[1:],
    )
    far_pieces = sent_round(far_masked)

    base = base_part(student, teacher, row_stats, [far_masked])
    near_inputs = (near_columns, near_stats, near_means)
    far_inputs = (far_columns, far_stats, far_means)
    grads = grad_part(
        place, near_inputs, near_pieces, None, 0, CHIP_IMAGES, F32, "grad_near", [base]
    )
    parts = pair_sum(pair_sum(parts, 2, 0), 4, 0)
    outgoing = grad_part(
        place, far_inputs, far_pieces, grads, IMAGES, IMAGES, BF16, "grad_far_sent", [parts]
    )
    incoming = swap_cores(outgoing)
    kept = grad_part(
        place, far_inputs, far_pieces, grads, 0, IMAGES, F32, "grad_far_kept", [outgoing], base
    )
    parts = four_sum(parts, (1, 0), (0, 1), add_four_kernel, "four_sum")
    gradient = kept + GRAD_SCALE * incoming.astype(F32)
    total_loss = four_sum(parts, (0, 2), (0, 4), loss_kernel, "loss", (1, 1), [gradient])
    return (gradient, total_loss[0, 0])


def solution(mesh):
    in_specs = (P("col", "row"), P("col", "row"))
    out_specs = (P("col", "row"), P())
    return jax.shard_map(
        per_device, mesh=mesh, in_specs=in_specs, out_specs=out_specs, check_vma=False
    )
```

```python
import functools

import jax
import jax.numpy as jnp
from jax import lax
from jax.experimental import pallas as pl
from jax.experimental.pallas import tpu as pltpu
from jax.sharding import PartitionSpec as P

F32 = jnp.float32
BF16 = jnp.bfloat16
IMAGES, FEATS, CHIPS = 768, 512, 8
BATCH = IMAGES * 16
CHIP_IMAGES = 2 * IMAGES
HALF = FEATS // 2
STAT_ROWS = 16
GRAD_SCALE = BATCH / (16.0 * (BATCH - 1))

QUARTER = FEATS // 4
UPPER = QUARTER // 2
VMEM = pl.BlockSpec(memory_space=pltpu.VMEM)
SMEM = pl.BlockSpec(memory_space=pltpu.SMEM)
ANY = pl.BlockSpec(memory_space=pl.ANY)


def shift_row(block, dx, dz):
    pairs = [(2 * x + z, 2 * ((x + dx) % 4) + (z + dz) % 2) for x in range(4) for z in range(2)]
    return lax.ppermute(block, "row", pairs)


def flip(block, z_lo, core):
    pairs = []
    for row in range(8):
        for col in range(16):
            pairs.append((16 * row + col, 16 * (row ^ z_lo) + (col ^ core)))
    return lax.ppermute(block, ("row", "col"), pairs)


def swap_cores(block):
    return lax.ppermute(block, "col", [(i, i ^ 1) for i in range(16)])


def shift_y(block, dy):
    pairs = [
        (8 * z + 2 * y + core, 8 * z + 2 * ((y + dy) % 4) + core)
        for z in range(2) for y in range(4) for core in range(2)
    ]
    return lax.ppermute(block, "col", pairs)


def sent_round(block):
    two, one, three_on = [shift_y(block, d) for d in (2, 1, 3)]
    return [block, one, two, three_on]


def swap_z_hi(block):
    return lax.ppermute(block, "col", [(i, i ^ 8) for i in range(16)])


def call(body, outs, ins, scratch, name, after=(), flops=0):
    count, waits = len(ins), len(after)

    def kernel(*refs):
        body(*refs[:count], *refs[count + waits:])

    return pl.pallas_call(
        kernel,
        out_shape=tuple(outs),
        in_specs=[SMEM if a.dtype == jnp.int32 else VMEM for a in ins] + [ANY] * waits,
        out_specs=tuple(VMEM for _ in outs),
        scratch_shapes=scratch,
        compiler_params=pltpu.CompilerParams(vmem_limit_bytes=16 * 2**20),
        cost_estimate=pl.CostEstimate(flops=flops, bytes_accessed=0, transcendentals=0),
        name=name,
    )(*ins, *after)


def shape(dims, dtype):
    return jax.ShapeDtypeStruct(dims, dtype)


def layout(chunks):
    places, column, at = [], 0, 0
    while at < len(chunks):
        rows, width = chunks[at].shape
        count = CHIP_IMAGES // rows
        for part in range(count):
            places.append((at + part, part * rows, column))
        column += width
        at += count
    return places, column


def split3(value):
    high = value.astype(BF16).astype(F32)
    middle = (value - high).astype(BF16).astype(F32)
    return [high, middle, value - high - middle]


def column_sum(ref):
    ones = jnp.ones((8, ref.shape[0]), BF16)
    return jnp.dot(ones, ref[...], preferred_element_type=F32)[0:1]


def center_into(target, first, column, ref, mean):
    width = ref.shape[1]
    step = 128

    def body(i, carry):
        at = pl.multiple_of(i * step, step)
        block = ref[pl.ds(at, step), :].astype(F32) - mean
        target[pl.ds(first + at, step), column:column + width] = block.astype(BF16)
        return carry

    lax.fori_loop(0, ref.shape[0] // step, body, 0)


def fill_columns(places, refs, columns, stats):
    means = {}
    for at, _, column in places:
        means[column] = means.get(column, 0.0) + column_sum(refs[at])
    for column, total in means.items():
        mean = total / CHIP_IMAGES
        stats[0:1, column:column + mean.shape[1]] = mean
        means[column] = mean
    for at, first, column in places:
        center_into(columns, first, column, refs[at], means[column])


def center_rows(target, first, ref, mean):
    step = 128

    def body(i, total):
        at = pl.multiple_of(i * step, step)
        block = ref[pl.ds(at, step), :].astype(F32) - mean
        target[pl.ds(first + at, step), :] = block.astype(BF16)
        return total + jnp.sum((block * block).reshape(step // 8, 8, FEATS), axis=0)

    total = lax.fori_loop(0, ref.shape[0] // step, body, jnp.zeros((8, FEATS), F32))
    return jnp.sum(total, axis=0, keepdims=True)


def padded(lines, width):
    pad = width - lines[0].shape[1]
    return [jnp.concatenate([line, jnp.zeros((line.shape[0], pad), F32)], axis=1) for line in lines]


def filled(lines, width):
    count = sum(line.shape[0] for line in lines)
    lines = lines + [jnp.zeros((-count % STAT_ROWS, width), F32)]
    return jnp.concatenate([line for line in lines if line.shape[0]], axis=0)


def rows_kernel(own, sibling, teacher, rows_t, row_stats, parts, rows):
    row_mean = (column_sum(own) + column_sum(sibling)) / CHIP_IMAGES
    squares = center_rows(rows, 0, own, row_mean) + center_rows(rows, IMAGES, sibling, row_mean)
    for at in range(0, FEATS, 128):
        rows_t[at:at + 128, :] = rows[:, at:at + 128].T
    row_stats[...] = jnp.concatenate([row_mean, squares, jnp.zeros((6, FEATS), F32)], axis=0)

    def body(i, total):
        at = pl.ds(pl.multiple_of(i * 128, 128), 128)
        diff = own[at, :].astype(F32) - teacher[at, :].astype(F32)
        return total + jnp.sum((diff * diff).reshape(16, 8, FEATS), axis=0)

    total = lax.fori_loop(0, IMAGES // 128, body, jnp.zeros((8, FEATS), F32))
    lanes = lax.broadcasted_iota(jnp.int32, parts.shape, 1)
    parts[...] = jnp.where(lanes == 1, jnp.sum(total, keepdims=True), 0.0)


def center_own(own, sibling, teacher, after):
    return call(
        rows_kernel,
        [shape((FEATS, CHIP_IMAGES), BF16), shape((8, FEATS), F32), shape((8, 128), F32)],
        [own, sibling, teacher],
        [pltpu.VMEM((CHIP_IMAGES, FEATS), BF16)],
        "center_own",
        after,
    )


def join_kernel(first, second, out):
    out[0:IMAGES, :] = first[...]
    out[IMAGES:CHIP_IMAGES, :] = second[...]


def join(first, second, after=()):
    return call(
        join_kernel, [shape((CHIP_IMAGES, HALF), BF16)], [first, second], [], "join", after
    )[0]


def base_kernel(student, teacher, row_stats, out):
    mean, spread = row_stats[0:1, :], row_stats[1:2, :]
    scale = jnp.where(spread < 1.0, 25.0 * BATCH / 64.0 / (spread * (BATCH - 1)), 0.0)

    def body(i, carry):
        at = pl.ds(pl.multiple_of(i * 64, 64), 64)
        value = student[at, :].astype(F32)
        diff = value - teacher[at, :].astype(F32)
        out[at, :] = (25.0 / 32.0) * diff - scale * (value - mean)
        return carry

    lax.fori_loop(0, IMAGES // 64, body, 0)


def base_part(student, teacher, row_stats, after):
    ins = [student, teacher, row_stats]
    return call(base_kernel, [shape((IMAGES, FEATS), F32)], ins, [], "base", after)[0]


def partial_kernel(places, width, count, with_rows, *refs):
    place, rows_t, row_stats = refs[:3]
    chunks = refs[3:3 + count]
    pieces = refs[3 + count:7 + count]
    columns, stats, sums = refs[7 + count:]
    fill_columns(places, chunks, columns, stats)
    for at in range(0, width, 256):
        sums[:, at:at + 256] = jnp.dot(
            rows_t[...], columns[:, at:at + 256], preferred_element_type=F32
        )
    lines = split3(stats[0:1, :])
    if with_rows:
        lines += padded(split3(row_stats[0:1, :]) + split3(row_stats[1:2, :]), width)
    block = filled(lines, width)
    for d in range(4):
        first = pl.multiple_of((place[2] + d) % 4 * QUARTER, QUARTER)
        pieces[d][0:QUARTER, :] = sums[pl.ds(first, QUARTER), :].astype(pieces[d].dtype)
        pieces[d][QUARTER:QUARTER + STAT_ROWS, :] = block.astype(pieces[d].dtype)


def partial_sums(place, rows_t, row_stats, chunks, with_rows, name, after=()):
    places, width = layout(chunks)
    rows = QUARTER + STAT_ROWS
    *pieces, columns, stats = call(
        functools.partial(partial_kernel, places, width, len(chunks), with_rows),
        [shape((rows, width), F32)]
        + [shape((rows, width), BF16)] * 3
        + [shape((CHIP_IMAGES, width), BF16), shape((8, width), F32)],
        [place, rows_t, row_stats] + chunks,
        [pltpu.VMEM((FEATS, width), F32)],
        name,
        after,
        flops=40 * CHIP_IMAGES * FEATS * width,
    )
    return pieces, columns, stats


def spread_out(local):
    mean = jnp.sum(local, axis=0, keepdims=True) / CHIPS
    return local - mean, mean


def mean_term(row_offsets, col_offsets):
    return CHIP_IMAGES * lax.dot_general(
        row_offsets,
        col_offsets,
        (((0,), (0,)), ((), ())),
        precision=lax.Precision.HIGHEST,
        preferred_element_type=F32,
    )


def three(stats, first):
    return stats[first:first + 1] + stats[first + 1:first + 2] + stats[first + 2:first + 3]


def combine_y_kernel(
    with_rows, place, parts, own, one, two, three_on, plane, message, local, *more
):
    width = own.shape[1]
    columns = jnp.zeros((4, width), F32)
    rows = jnp.zeros((4, FEATS), F32)
    squares = jnp.zeros((1, FEATS), F32)
    total = own[0:QUARTER, :]
    for d, piece in enumerate((own, one, two, three_on)):
        if d:
            total = total + piece[0:QUARTER, :].astype(F32)
        at = (place[2] + 4 - d) % 4
        stats = piece[QUARTER:QUARTER + STAT_ROWS, :].astype(F32)
        here = lax.broadcasted_iota(jnp.int32, columns.shape, 0) == at
        columns = jnp.where(here, three(stats, 0), columns)
        if with_rows:
            here = lax.broadcasted_iota(jnp.int32, rows.shape, 0) == at
            rows = jnp.where(here, three(stats[:, 0:FEATS], 3), rows)
            squares = squares + three(stats[:, 0:FEATS], 6)

    def rounded(value):
        high, middle, low = split3(value)
        low = low.astype(BF16).astype(F32)
        return [high, middle, low], high + middle + low

    plane[...] = total.astype(BF16)
    upper = 0 if with_rows else UPPER
    message[0:QUARTER - upper, :] = total[upper:].astype(BF16)
    if upper:
        more[0][...] = total[0:upper].astype(BF16)
    lines, local[0:4, :] = rounded(columns)
    if with_rows:
        row_lines, more[0][0:4, :] = rounded(rows)
        square_lines, more[0][4:5, :] = rounded(squares)
        part_lines, _ = rounded(parts[0:1, :])
        lines = lines + padded(row_lines + square_lines, width) + padded(part_lines, width)
    block = filled(lines, width)
    message[QUARTER - upper:, :] = block.astype(BF16)


def combine_y(place, parts, pieces, with_rows, name, after=()):
    width = pieces[0].shape[1]
    rows = QUARTER + 2 * STAT_ROWS if with_rows else QUARTER - UPPER + STAT_ROWS
    outs = [shape((QUARTER, width), BF16), shape((rows, width), BF16), shape((8, width), F32)]
    outs.append(shape((8, FEATS), F32) if with_rows else shape((UPPER, width), BF16))
    return call(
        functools.partial(combine_y_kernel, with_rows), outs, [place, parts] + pieces, [], name, after
    )


def all_chips(place, mine, theirs):
    low = place[3] == 0
    return jnp.concatenate([jnp.where(low, mine, theirs), jnp.where(low, theirs, mine)], axis=0)


def combine_z_kernel(
    with_rows, place, plane, local, rows, parts, received, *more
):
    upper = 0 if with_rows else UPPER
    if not with_rows:
        other_upper, *more = more
    masked, part, means, *more = more
    stats = received[QUARTER - upper:, :].astype(F32)
    theirs = stats[0:4] + stats[4:8] + stats[8:12]
    col_off, col_mean = spread_out(all_chips(place, local[0:4, :], theirs))
    means[...] = jnp.broadcast_to(col_mean, means.shape)
    row_offsets = rows
    if with_rows:
        row_offsets, row_stats = more
        other_parts = three(stats[:, 0:128], 27)
        stats = stats[:, 0:FEATS]
        theirs = stats[12:16] + stats[16:20] + stats[20:24]
        row_off, row_mean = spread_out(all_chips(place, rows[0:4, :], theirs))
        squares = rows[4:5, :] + three(stats, 24)
        squares = squares + CHIP_IMAGES * jnp.sum(row_off * row_off, axis=0, keepdims=True)
        variance = squares / (BATCH - 1)
        row_offsets[...] = row_off
        spread = jnp.sqrt(variance + 0.0001)
        row_stats[...] = jnp.concatenate([row_mean, spread, jnp.zeros((6, FEATS), F32)], axis=0)
    block = pl.multiple_of(place[2] * QUARTER, QUARTER)
    term = mean_term(row_offsets[:, pl.ds(block, QUARTER)], col_off)
    other = received[0:QUARTER - upper, :].astype(F32)
    if upper:
        other = jnp.concatenate([other_upper[...].astype(F32), other], axis=0)
    covar = plane[...].astype(F32) + other
    covar = (covar + term) / (BATCH - 1)
    if with_rows:
        row_ids = place[2] * QUARTER + lax.broadcasted_iota(jnp.int32, covar.shape, 0)
        col_ids = lax.broadcasted_iota(jnp.int32, covar.shape, 1)
        on_diagonal = (col_ids < HALF) & (row_ids == col_ids + place[1] * HALF)
        covar = jnp.where(on_diagonal, F32(0.0), covar)
    lanes = lax.broadcasted_iota(jnp.int32, part.shape, 1)
    found = jnp.where(lanes == 0, jnp.sum(covar * covar, keepdims=True), 0.0)
    if with_rows:
        var_part = jnp.sum(jnp.maximum(0.0, 1.0 - spread), keepdims=True) / 8
        found = found + jnp.where(lanes == 2, var_part, 0.0) + other_parts
    part[...] = parts[...] + found
    masked[0:QUARTER, :] = covar.astype(BF16)


def combine_z(place, plane, local, rows, parts, received, with_rows, name, after=()):
    width = plane.shape[1]
    outs = [shape((QUARTER, width), BF16), shape((8, 128), F32), shape((8, width), F32)]
    outs += [shape((8, FEATS), F32)] * 2 if with_rows else []
    ins = [place, plane, local, rows, parts] + received
    return call(functools.partial(combine_z_kernel, with_rows), outs, ins, [], name, after)


def add_kernel(one, two, out):
    out[...] = one[...] + two[...]


def add_four_kernel(one, two, three_on, four, out):
    out[...] = (one[...] + two[...]) + (three_on[...] + four[...])


def loss_kernel(one, two, three_on, four, out):
    total = (one[...] + two[...]) + (three_on[...] + four[...])
    loss = total[0:1, 0:1] + 25.0 * (total[0:1, 1:2] / BATCH + total[0:1, 2:3])
    out[...] = loss / (8 * FEATS)


def flip(parts, row_bits, col_bits):
    if not row_bits:
        return lax.ppermute(parts, "col", [(i, i ^ col_bits) for i in range(16)])
    if not col_bits:
        return lax.ppermute(parts, "row", [(i, i ^ row_bits) for i in range(8)])
    pairs = [
        (16 * row + col, 16 * (row ^ row_bits) + (col ^ col_bits))
        for row in range(8) for col in range(16)
    ]
    return lax.ppermute(parts, ("row", "col"), pairs)


def pair_sum(parts, row_bits, col_bits, after=()):
    ins = [parts, flip(parts, row_bits, col_bits)]
    return call(add_kernel, [shape((8, 128), F32)], ins, [], "pair_sum", after)[0]


def four_sum(parts, first, second, body, name, out=(8, 128), after=()):
    both = (first[0] | second[0], first[1] | second[1])
    ins = [parts] + [flip(parts, *bits) for bits in (first, second, both)]
    return call(body, [shape(out, F32)], ins, [], name, after)[0]


def shift_term(stats, means, masked):
    lines = filled(split3(stats[0:1, :] - means[0:1, :]), stats.shape[1]).astype(BF16)
    rows = lax.dot_general(
        lines, masked[...], (((1,), (1,)), ((), ())), preferred_element_type=F32
    )
    return rows[0:1] + rows[1:2] + rows[2:3]


def times_masked(columns, at, masked):
    return lax.dot_general(
        columns[at:at + 256, :], masked[...], (((1,), (1,)), ((), ())), preferred_element_type=F32
    )


def grad_kernel(
    first, rows, add, with_base, place, columns, stats, means, own, one, two, three_on, *rest
):
    out, masked = rest[-2:]
    for d, piece in enumerate((own, one, two, three_on)):
        row = pl.multiple_of((place[2] + 4 - d) % 4 * QUARTER, QUARTER)
        masked[pl.ds(row, QUARTER), :] = piece[0:QUARTER, :]
    shift = shift_term(stats, means, masked)
    for at in range(first, first + rows, 256):
        product = times_masked(columns, at, masked) + shift
        if add:
            product = product + rest[0][at:at + 256, :]
        if with_base:
            product = GRAD_SCALE * product + rest[1][at:at + 256, :]
        out[at - first:at - first + 256, :] = product.astype(out.dtype)


def grad_part(place, inputs, pieces, previous, first, rows, dtype, name, after=(), base=None):
    columns, stats, means = inputs
    ins = [place, columns, stats, means] + pieces
    ins += [a for a in (previous, base) if a is not None]
    return call(
        functools.partial(
            grad_kernel, first, rows, previous is not None, base is not None
        ),
        [shape((rows, FEATS), dtype)],
        ins,
        [pltpu.VMEM((FEATS, columns.shape[1]), BF16)],
        name,
        after,
    )[0]


def per_device(student, teacher):
    row_index = lax.axis_index("row")
    col_index = lax.axis_index("col")
    core = col_index % 2
    chip = col_index // 2
    place = jnp.stack([chip, core, chip % 4, chip // 4, row_index // 2]).astype(jnp.int32)

    sibling = swap_cores(student)
    own_a = lax.dynamic_slice_in_dim(student, core * HALF, HALF, 1)
    x_lo_a = shift_row(own_a, 1, 0)
    x_hi_a = shift_row(own_a, -1, 0)
    own_b = lax.dynamic_slice_in_dim(sibling, core * HALF, HALF, 1)
    x_lo_b = shift_row(own_b, 1, 0)
    x_hi_b = shift_row(own_b, -1, 0)
    z_own_a = shift_row(own_a, 0, 1)
    z_own_b = shift_row(own_b, 0, 1)
    rows_t, own_stats, parts = center_own(student, sibling, teacher, [x_lo_a])
    x_next, own_stats = lax.optimization_barrier((x_lo_a, own_stats))
    x_far_a = shift_row(x_next, 1, 0)
    x_far_b = shift_row(x_hi_b, -1, 0)
    near = [own_a, own_b, x_lo_a, x_lo_b, x_hi_a, x_hi_b, z_own_a, z_own_b]

    near_sums, near_columns, near_stats = partial_sums(
        place, rows_t, own_stats, near, True, "partial_near"
    )
    z_own = join(z_own_a, z_own_b, [near_stats])
    z_lo = shift_row(z_own, 1, 0)
    z_hi = shift_row(z_own, -1, 0)
    x_far = join(x_far_a, x_far_b, [z_own])
    z_far = shift_row(x_far, 0, 1)
    far = [x_far, z_lo, z_hi, z_far]
    near_sums[1], near_sums[3] = shift_y(near_sums[1], 1), shift_y(near_sums[3], 3)
    near_sums = list(lax.optimization_barrier(tuple(near_sums)))
    near_sums[2] = shift_y(near_sums[2], 2)
    far_sums, far_columns, far_stats = partial_sums(
        place, rows_t, own_stats, far, False, "partial_far"
    )
    plane, message, local, row_local = combine_y(
        place, parts, near_sums, True, "combine_y_near", [far_sums[0]]
    )
    for d in (1, 3, 2):
        far_sums[d] = shift_y(far_sums[d], d)
    near_masked, parts, near_means, row_offsets, row_stats = combine_z(
        place, plane, local, row_local, parts, [swap_z_hi(message)], True, "combine_z_near",
        [far_sums[1]],
    )
    near_pieces = sent_round(near_masked)
    far_plane, far_message, far_local, far_upper = combine_y(
        place, parts, far_sums, False, "combine_y_far", [near_masked]
    )
    far_masked, parts, far_means = combine_z(
        place, far_plane, far_local, row_offsets, parts,
        [swap_z_hi(far_message), swap_z_hi(far_upper)], False, "combine_z_far", [near_pieces[1], near_pieces[3]],
    )
    far_pieces = sent_round(far_masked)

    base = base_part(student, teacher, row_stats, [far_masked])
    near_inputs = (near_columns, near_stats, near_means)
    far_inputs = (far_columns, far_stats, far_means)
    grads = grad_part(
        place, near_inputs, near_pieces, None, 0, CHIP_IMAGES, F32, "grad_near", [base]
    )
    parts = pair_sum(pair_sum(parts, 2, 0), 4, 0)
    outgoing = grad_part(
        place, far_inputs, far_pieces, grads, IMAGES, IMAGES, BF16, "grad_far_sent", [parts]
    )
    incoming = swap_cores(outgoing)
    kept = grad_part(
        place, far_inputs, far_pieces, grads, 0, IMAGES, F32, "grad_far_kept", [outgoing], base
    )
    parts = four_sum(parts, (1, 0), (0, 1), add_four_kernel, "four_sum")
    gradient = kept + GRAD_SCALE * incoming.astype(F32)
    total_loss = four_sum(parts, (0, 2), (0, 4), loss_kernel, "loss", (1, 1), [gradient])
    return (gradient, total_loss[0, 0])


def solution(mesh):
    in_specs = (P("col", "row"), P("col", "row"))
    out_specs = (P("col", "row"), P())
    return jax.shard_map(
        per_device, mesh=mesh, in_specs=in_specs, out_specs=out_specs, check_vma=False
    )
```

```python
import functools

import jax
import jax.numpy as jnp
from jax import lax
from jax.experimental import pallas as pl
from jax.experimental.pallas import tpu as pltpu
from jax.sharding import PartitionSpec as P

F32 = jnp.float32
BF16 = jnp.bfloat16
IMAGES, FEATS, CHIPS = 768, 512, 8
BATCH = IMAGES * 16
CHIP_IMAGES = 2 * IMAGES
HALF = FEATS // 2
STAT_ROWS = 16
GRAD_SCALE = BATCH / (16.0 * (BATCH - 1))

QUARTER = FEATS // 4
UPPER = QUARTER // 2
VMEM = pl.BlockSpec(memory_space=pltpu.VMEM)
SMEM = pl.BlockSpec(memory_space=pltpu.SMEM)
ANY = pl.BlockSpec(memory_space=pl.ANY)


def shift_row(block, dx, dz):
    pairs = [(2 * x + z, 2 * ((x + dx) % 4) + (z + dz) % 2) for x in range(4) for z in range(2)]
    return lax.ppermute(block, "row", pairs)


def flip(block, z_lo, core):
    pairs = []
    for row in range(8):
        for col in range(16):
            pairs.append((16 * row + col, 16 * (row ^ z_lo) + (col ^ core)))
    return lax.ppermute(block, ("row", "col"), pairs)


def swap_cores(block):
    return lax.ppermute(block, "col", [(i, i ^ 1) for i in range(16)])


def shift_y(block, dy):
    pairs = [
        (8 * z + 2 * y + core, 8 * z + 2 * ((y + dy) % 4) + core)
        for z in range(2) for y in range(4) for core in range(2)
    ]
    return lax.ppermute(block, "col", pairs)


def sent_round(block):
    two, one, three_on = [shift_y(block, d) for d in (2, 1, 3)]
    return [block, one, two, three_on]


def swap_z_hi(block):
    return lax.ppermute(block, "col", [(i, i ^ 8) for i in range(16)])


def call(body, outs, ins, scratch, name, after=(), flops=0):
    count, waits = len(ins), len(after)

    def kernel(*refs):
        body(*refs[:count], *refs[count + waits:])

    return pl.pallas_call(
        kernel,
        out_shape=tuple(outs),
        in_specs=[SMEM if a.dtype == jnp.int32 else VMEM for a in ins] + [ANY] * waits,
        out_specs=tuple(VMEM for _ in outs),
        scratch_shapes=scratch,
        compiler_params=pltpu.CompilerParams(vmem_limit_bytes=16 * 2**20),
        cost_estimate=pl.CostEstimate(flops=flops, bytes_accessed=0, transcendentals=0),
        name=name,
    )(*ins, *after)


def shape(dims, dtype):
    return jax.ShapeDtypeStruct(dims, dtype)


def layout(chunks):
    places, column, at = [], 0, 0
    while at < len(chunks):
        rows, width = chunks[at].shape
        count = CHIP_IMAGES // rows
        for part in range(count):
            places.append((at + part, part * rows, column))
        column += width
        at += count
    return places, column


def split3(value):
    high = value.astype(BF16).astype(F32)
    middle = (value - high).astype(BF16).astype(F32)
    return [high, middle, value - high - middle]


def column_sum(ref):
    ones = jnp.ones((8, ref.shape[0]), BF16)
    return jnp.dot(ones, ref[...], preferred_element_type=F32)[0:1]


def center_into(target, first, column, ref, mean):
    width = ref.shape[1]
    step = 128

    def body(i, carry):
        at = pl.multiple_of(i * step, step)
        block = ref[pl.ds(at, step), :].astype(F32) - mean
        target[pl.ds(first + at, step), column:column + width] = block.astype(BF16)
        return carry

    lax.fori_loop(0, ref.shape[0] // step, body, 0)


def fill_columns(places, refs, columns, stats):
    means = {}
    for at, _, column in places:
        means[column] = means.get(column, 0.0) + column_sum(refs[at])
    for column, total in means.items():
        mean = total / CHIP_IMAGES
        stats[0:1, column:column + mean.shape[1]] = mean
        means[column] = mean
    for at, first, column in places:
        center_into(columns, first, column, refs[at], means[column])


def center_rows(target, first, ref, mean):
    step = 128

    def body(i, total):
        at = pl.multiple_of(i * step, step)
        block = ref[pl.ds(at, step), :].astype(F32) - mean
        target[pl.ds(first + at, step), :] = block.astype(BF16)
        return total + jnp.sum((block * block).reshape(step // 8, 8, FEATS), axis=0)

    total = lax.fori_loop(0, ref.shape[0] // step, body, jnp.zeros((8, FEATS), F32))
    return jnp.sum(total, axis=0, keepdims=True)


def padded(lines, width):
    pad = width - lines[0].shape[1]
    return [jnp.concatenate([line, jnp.zeros((line.shape[0], pad), F32)], axis=1) for line in lines]


def filled(lines, width):
    count = sum(line.shape[0] for line in lines)
    lines = lines + [jnp.zeros((-count % STAT_ROWS, width), F32)]
    return jnp.concatenate([line for line in lines if line.shape[0]], axis=0)


def rows_kernel(own, sibling, teacher, rows_t, row_stats, parts, rows):
    row_mean = (column_sum(own) + column_sum(sibling)) / CHIP_IMAGES
    squares = center_rows(rows, 0, own, row_mean) + center_rows(rows, IMAGES, sibling, row_mean)
    for at in range(0, FEATS, 128):
        rows_t[at:at + 128, :] = rows[:, at:at + 128].T
    row_stats[...] = jnp.concatenate([row_mean, squares, jnp.zeros((6, FEATS), F32)], axis=0)

    def body(i, total):
        at = pl.ds(pl.multiple_of(i * 128, 128), 128)
        diff = own[at, :].astype(F32) - teacher[at, :].astype(F32)
        return total + jnp.sum((diff * diff).reshape(16, 8, FEATS), axis=0)

    total = lax.fori_loop(0, IMAGES // 128, body, jnp.zeros((8, FEATS), F32))
    lanes = lax.broadcasted_iota(jnp.int32, parts.shape, 1)
    parts[...] = jnp.where(lanes == 1, jnp.sum(total, keepdims=True), 0.0)


def center_own(own, sibling, teacher, after):
    return call(
        rows_kernel,
        [shape((FEATS, CHIP_IMAGES), BF16), shape((8, FEATS), F32), shape((8, 128), F32)],
        [own, sibling, teacher],
        [pltpu.VMEM((CHIP_IMAGES, FEATS), BF16)],
        "center_own",
        after,
    )


def join_kernel(first, second, out):
    out[0:IMAGES, :] = first[...]
    out[IMAGES:CHIP_IMAGES, :] = second[...]


def join(first, second, after=()):
    return call(
        join_kernel, [shape((CHIP_IMAGES, HALF), BF16)], [first, second], [], "join", after
    )[0]


def base_kernel(student, teacher, row_stats, out):
    mean, spread = row_stats[0:1, :], row_stats[1:2, :]
    scale = jnp.where(spread < 1.0, 25.0 * BATCH / 64.0 / (spread * (BATCH - 1)), 0.0)

    def body(i, carry):
        at = pl.ds(pl.multiple_of(i * 64, 64), 64)
        value = student[at, :].astype(F32)
        diff = value - teacher[at, :].astype(F32)
        out[at, :] = (25.0 / 32.0) * diff - scale * (value - mean)
        return carry

    lax.fori_loop(0, IMAGES // 64, body, 0)


def base_part(student, teacher, row_stats, after):
    ins = [student, teacher, row_stats]
    return call(base_kernel, [shape((IMAGES, FEATS), F32)], ins, [], "base", after)[0]


def partial_kernel(places, width, count, with_rows, *refs):
    place, rows_t, row_stats = refs[:3]
    chunks = refs[3:3 + count]
    pieces = refs[3 + count:7 + count]
    columns, stats, sums = refs[7 + count:]
    fill_columns(places, chunks, columns, stats)
    for at in range(0, width, 256):
        sums[:, at:at + 256] = jnp.dot(
            rows_t[...], columns[:, at:at + 256], preferred_element_type=F32
        )
    lines = split3(stats[0:1, :])
    if with_rows:
        lines += padded(split3(row_stats[0:1, :]) + split3(row_stats[1:2, :]), width)
    block = filled(lines, width)
    for d in range(4):
        first = pl.multiple_of((place[2] + d) % 4 * QUARTER, QUARTER)
        pieces[d][0:QUARTER, :] = sums[pl.ds(first, QUARTER), :].astype(pieces[d].dtype)
        pieces[d][QUARTER:QUARTER + STAT_ROWS, :] = block.astype(pieces[d].dtype)


def partial_sums(place, rows_t, row_stats, chunks, with_rows, name, after=()):
    places, width = layout(chunks)
    rows = QUARTER + STAT_ROWS
    *pieces, columns, stats = call(
        functools.partial(partial_kernel, places, width, len(chunks), with_rows),
        [shape((rows, width), F32)]
        + [shape((rows, width), BF16)] * 3
        + [shape((CHIP_IMAGES, width), BF16), shape((8, width), F32)],
        [place, rows_t, row_stats] + chunks,
        [pltpu.VMEM((FEATS, width), F32)],
        name,
        after,
        flops=40 * CHIP_IMAGES * FEATS * width,
    )
    return pieces, columns, stats


def spread_out(local):
    mean = jnp.sum(local, axis=0, keepdims=True) / CHIPS
    return local - mean, mean


def mean_term(row_offsets, col_offsets):
    return CHIP_IMAGES * lax.dot_general(
        row_offsets,
        col_offsets,
        (((0,), (0,)), ((), ())),
        precision=lax.Precision.HIGHEST,
        preferred_element_type=F32,
    )


def three(stats, first):
    return stats[first:first + 1] + stats[first + 1:first + 2] + stats[first + 2:first + 3]


def combine_y_kernel(
    with_rows, place, parts, own, one, two, three_on, plane, upper, message, local, *row_local
):
    width = own.shape[1]
    columns = jnp.zeros((4, width), F32)
    rows = jnp.zeros((4, FEATS), F32)
    squares = jnp.zeros((1, FEATS), F32)
    total = own[0:QUARTER, :]
    for d, piece in enumerate((own, one, two, three_on)):
        if d:
            total = total + piece[0:QUARTER, :].astype(F32)
        at = (place[2] + 4 - d) % 4
        stats = piece[QUARTER:QUARTER + STAT_ROWS, :].astype(F32)
        here = lax.broadcasted_iota(jnp.int32, columns.shape, 0) == at
        columns = jnp.where(here, three(stats, 0), columns)
        if with_rows:
            here = lax.broadcasted_iota(jnp.int32, rows.shape, 0) == at
            rows = jnp.where(here, three(stats[:, 0:FEATS], 3), rows)
            squares = squares + three(stats[:, 0:FEATS], 6)

    def rounded(value):
        high, middle, low = split3(value)
        low = low.astype(BF16).astype(F32)
        return [high, middle, low], high + middle + low

    plane[...] = total.astype(BF16)
    upper[...] = total[0:UPPER].astype(BF16)
    message[0:QUARTER - UPPER, :] = total[UPPER:].astype(BF16)
    lines, local[0:4, :] = rounded(columns)
    if with_rows:
        row_lines, row_local[0][0:4, :] = rounded(rows)
        square_lines, row_local[0][4:5, :] = rounded(squares)
        part_lines, _ = rounded(parts[0:1, :])
        lines = lines + padded(row_lines + square_lines, width) + padded(part_lines, width)
    block = filled(lines, width)
    message[QUARTER - UPPER:, :] = block.astype(BF16)


def combine_y(place, parts, pieces, with_rows, name, after=()):
    width = pieces[0].shape[1]
    rows = QUARTER - UPPER + (2 if with_rows else 1) * STAT_ROWS
    outs = [shape((QUARTER, width), BF16), shape((UPPER, width), BF16)]
    outs += [shape((rows, width), BF16), shape((8, width), F32)]
    outs += [shape((8, FEATS), F32)] if with_rows else []
    return call(
        functools.partial(combine_y_kernel, with_rows), outs, [place, parts] + pieces, [], name, after
    )


def all_chips(place, mine, theirs):
    low = place[3] == 0
    return jnp.concatenate([jnp.where(low, mine, theirs), jnp.where(low, theirs, mine)], axis=0)


def combine_z_kernel(
    with_rows, place, plane, local, rows, upper, received, parts, masked, part, means, *more
):
    stats = received[QUARTER - UPPER:, :].astype(F32)
    theirs = stats[0:4] + stats[4:8] + stats[8:12]
    col_off, col_mean = spread_out(all_chips(place, local[0:4, :], theirs))
    means[...] = jnp.broadcast_to(col_mean, means.shape)
    row_offsets = rows
    if with_rows:
        row_offsets, row_stats = more
        other_parts = three(stats[:, 0:128], 27)
        stats = stats[:, 0:FEATS]
        theirs = stats[12:16] + stats[16:20] + stats[20:24]
        row_off, row_mean = spread_out(all_chips(place, rows[0:4, :], theirs))
        squares = rows[4:5, :] + three(stats, 24)
        squares = squares + CHIP_IMAGES * jnp.sum(row_off * row_off, axis=0, keepdims=True)
        variance = squares / (BATCH - 1)
        row_offsets[...] = row_off
        spread = jnp.sqrt(variance + 0.0001)
        row_stats[...] = jnp.concatenate([row_mean, spread, jnp.zeros((6, FEATS), F32)], axis=0)
    block = pl.multiple_of(place[2] * QUARTER, QUARTER)
    term = mean_term(row_offsets[:, pl.ds(block, QUARTER)], col_off)
    other = [upper[...].astype(F32), received[0:QUARTER - UPPER, :].astype(F32)]
    covar = plane[...].astype(F32) + jnp.concatenate(other, axis=0)
    covar = (covar + term) / (BATCH - 1)
    if with_rows:
        row_ids = place[2] * QUARTER + lax.broadcasted_iota(jnp.int32, covar.shape, 0)
        col_ids = lax.broadcasted_iota(jnp.int32, covar.shape, 1)
        on_diagonal = (col_ids < HALF) & (row_ids == col_ids + place[1] * HALF)
        covar = jnp.where(on_diagonal, F32(0.0), covar)
    lanes = lax.broadcasted_iota(jnp.int32, part.shape, 1)
    found = jnp.where(lanes == 0, jnp.sum(covar * covar, keepdims=True), 0.0)
    if with_rows:
        var_part = jnp.sum(jnp.maximum(0.0, 1.0 - spread), keepdims=True) / 8
        found = found + jnp.where(lanes == 2, var_part, 0.0) + other_parts
    part[...] = parts[...] + found
    masked[0:QUARTER, :] = covar.astype(BF16)


def combine_z(place, plane, local, rows, upper, received, parts, with_rows, name, after=()):
    width = plane.shape[1]
    outs = [shape((QUARTER, width), BF16), shape((8, 128), F32), shape((8, width), F32)]
    outs += [shape((8, FEATS), F32)] * 2 if with_rows else []
    ins = [place, plane, local, rows, upper, received, parts]
    return call(functools.partial(combine_z_kernel, with_rows), outs, ins, [], name, after)


def add_kernel(one, two, out):
    out[...] = one[...] + two[...]


def add_four_kernel(one, two, three_on, four, out):
    out[...] = (one[...] + two[...]) + (three_on[...] + four[...])


def loss_kernel(one, two, three_on, four, out):
    total = (one[...] + two[...]) + (three_on[...] + four[...])
    loss = total[0:1, 0:1] + 25.0 * (total[0:1, 1:2] / BATCH + total[0:1, 2:3])
    out[...] = loss / (8 * FEATS)


def flip(parts, row_bits, col_bits):
    if not row_bits:
        return lax.ppermute(parts, "col", [(i, i ^ col_bits) for i in range(16)])
    if not col_bits:
        return lax.ppermute(parts, "row", [(i, i ^ row_bits) for i in range(8)])
    pairs = [
        (16 * row + col, 16 * (row ^ row_bits) + (col ^ col_bits))
        for row in range(8) for col in range(16)
    ]
    return lax.ppermute(parts, ("row", "col"), pairs)


def pair_sum(parts, row_bits, col_bits, after=()):
    ins = [parts, flip(parts, row_bits, col_bits)]
    return call(add_kernel, [shape((8, 128), F32)], ins, [], "pair_sum", after)[0]


def four_sum(parts, first, second, body, name, out=(8, 128), after=()):
    both = (first[0] | second[0], first[1] | second[1])
    ins = [parts] + [flip(parts, *bits) for bits in (first, second, both)]
    return call(body, [shape(out, F32)], ins, [], name, after)[0]


def shift_term(stats, means, masked):
    lines = filled(split3(stats[0:1, :] - means[0:1, :]), stats.shape[1]).astype(BF16)
    rows = lax.dot_general(
        lines, masked[...], (((1,), (1,)), ((), ())), preferred_element_type=F32
    )
    return rows[0:1] + rows[1:2] + rows[2:3]


def times_masked(columns, at, masked):
    return lax.dot_general(
        columns[at:at + 256, :], masked[...], (((1,), (1,)), ((), ())), preferred_element_type=F32
    )


def grad_kernel(
    first, rows, add, with_base, place, columns, stats, means, own, one, two, three_on, *rest
):
    out, masked = rest[-2:]
    for d, piece in enumerate((own, one, two, three_on)):
        row = pl.multiple_of((place[2] + 4 - d) % 4 * QUARTER, QUARTER)
        masked[pl.ds(row, QUARTER), :] = piece[0:QUARTER, :]
    shift = shift_term(stats, means, masked)
    for at in range(first, first + rows, 256):
        product = times_masked(columns, at, masked) + shift
        if add:
            product = product + rest[0][at:at + 256, :]
        if with_base:
            product = GRAD_SCALE * product + rest[1][at:at + 256, :]
        out[at - first:at - first + 256, :] = product.astype(out.dtype)


def grad_part(place, inputs, pieces, previous, first, rows, dtype, name, after=(), base=None):
    columns, stats, means = inputs
    ins = [place, columns, stats, means] + pieces
    ins += [a for a in (previous, base) if a is not None]
    return call(
        functools.partial(
            grad_kernel, first, rows, previous is not None, base is not None
        ),
        [shape((rows, FEATS), dtype)],
        ins,
        [pltpu.VMEM((FEATS, columns.shape[1]), BF16)],
        name,
        after,
    )[0]


def per_device(student, teacher):
    row_index = lax.axis_index("row")
    col_index = lax.axis_index("col")
    core = col_index % 2
    chip = col_index // 2
    place = jnp.stack([chip, core, chip % 4, chip // 4, row_index // 2]).astype(jnp.int32)

    sibling = swap_cores(student)
    own_a = lax.dynamic_slice_in_dim(student, core * HALF, HALF, 1)
    x_lo_a = shift_row(own_a, 1, 0)
    x_hi_a = shift_row(own_a, -1, 0)
    own_b = lax.dynamic_slice_in_dim(sibling, core * HALF, HALF, 1)
    x_lo_b = shift_row(own_b, 1, 0)
    x_hi_b = shift_row(own_b, -1, 0)
    z_own_a = shift_row(own_a, 0, 1)
    z_own_b = shift_row(own_b, 0, 1)
    rows_t, own_stats, parts = center_own(student, sibling, teacher, [x_lo_a])
    x_next, own_stats = lax.optimization_barrier((x_lo_a, own_stats))
    x_far_a = shift_row(x_next, 1, 0)
    x_far_b = shift_row(x_hi_b, -1, 0)
    near = [own_a, own_b, x_lo_a, x_lo_b, x_hi_a, x_hi_b, z_own_a, z_own_b]

    near_sums, near_columns, near_stats = partial_sums(
        place, rows_t, own_stats, near, True, "partial_near"
    )
    z_own = join(z_own_a, z_own_b, [near_stats])
    z_lo = shift_row(z_own, 1, 0)
    z_hi = shift_row(z_own, -1, 0)
    x_far = join(x_far_a, x_far_b, [z_own])
    z_far = shift_row(x_far, 0, 1)
    far = [x_far, z_lo, z_hi, z_far]
    near_sums[1], near_sums[3] = shift_y(near_sums[1], 1), shift_y(near_sums[3], 3)
    near_sums = list(lax.optimization_barrier(tuple(near_sums)))
    near_sums[2] = shift_y(near_sums[2], 2)
    far_sums, far_columns, far_stats = partial_sums(
        place, rows_t, own_stats, far, False, "partial_far"
    )
    plane, upper, message, local, row_local = combine_y(
        place, parts, near_sums, True, "combine_y_near", [far_sums[0]]
    )
    *far_sums, plane = lax.optimization_barrier((*far_sums, plane))
    for d in (1, 3, 2):
        far_sums[d] = shift_y(far_sums[d], d)
    near_masked, parts, near_means, row_offsets, row_stats = combine_z(
        place, plane, local, row_local, swap_z_hi(upper), swap_z_hi(message), parts, True,
        "combine_z_near", [far_sums[1]],
    )
    near_pieces = sent_round(near_masked)
    far_plane, far_upper, far_message, far_local = combine_y(
        place, parts, far_sums, False, "combine_y_far", [near_masked]
    )
    far_masked, parts, far_means = combine_z(
        place, far_plane, far_local, row_offsets, swap_z_hi(far_upper), swap_z_hi(far_message),
        parts, False,
        "combine_z_far", [near_pieces[1], near_pieces[3]],
    )
    far_pieces = sent_round(far_masked)

    base = base_part(student, teacher, row_stats, [far_masked])
    near_inputs = (near_columns, near_stats, near_means)
    far_inputs = (far_columns, far_stats, far_means)
    grads = grad_part(
        place, near_inputs, near_pieces, None, 0, CHIP_IMAGES, F32, "grad_near", [base]
    )
    parts = pair_sum(pair_sum(parts, 2, 0), 4, 0)
    outgoing = grad_part(
        place, far_inputs, far_pieces, grads, IMAGES, IMAGES, BF16, "grad_far_sent", [parts]
    )
    incoming = swap_cores(outgoing)
    kept = grad_part(
        place, far_inputs, far_pieces, grads, 0, IMAGES, F32, "grad_far_kept", [outgoing], base
    )
    parts = four_sum(parts, (1, 0), (0, 1), add_four_kernel, "four_sum")
    gradient = kept + GRAD_SCALE * incoming.astype(F32)
    total_loss = four_sum(parts, (0, 2), (0, 4), loss_kernel, "loss", (1, 1), [gradient])
    return (gradient, total_loss[0, 0])


def solution(mesh):
    in_specs = (P("col", "row"), P("col", "row"))
    out_specs = (P("col", "row"), P())
    return jax.shard_map(
        per_device, mesh=mesh, in_specs=in_specs, out_specs=out_specs, check_vma=False
    )
```
